512 devices in a mesh: seg: 8 (over z_hi, core), op: 64 (over x, z_lo, y).
Axes of the slice: x: 4, y: 8, z: 8 (z_hi: 4, z_lo: 2; z = z_hi * 2 + z_lo), core: 2. Of those that a mesh axis runs over, the one named last changes fastest.
Arguments:
- site_tensor: bfloat16 [8, 3, 4096, 128], P('seg'), may hold values from -0.375 to 0.375
- term_ops: bfloat16 [64, 4096, 128], P('op'), may hold values from -6 to 6
- env_rows: bfloat16 [4096, 128], P('op'), may hold values from -6 to 6
- term_shift: int32 [64], P('op'), may hold values from -1 to 1
- keep_weight: float32 [64, 3], P('op'), may hold values from 0.6 to 1.4
- env_weight: float32 [64, 3], P('op'), may hold values from -0.4375 to 0.4375
Outputs:
- bond_env: bfloat16 [8, 4096, 128], P('seg', 'op')
The draws below stay inside these ranges and needn't reach their ends.
Inputs may be any that keep to these rules, and one draw needn't show every extreme that they name: term_shift[t] is the sector change of term t.
All inputs are finite; a program needn't handle non-finite values.
Results may differ from the reference program's by a relative error of at most 0.025.
Values may be sent and summed in bfloat16 or wider, within the bound.
No kernel may reach another device: no remote copies, remote signals or barrier semaphores. Data moves between devices by JAX's collectives and lax.ppermute only.
A program may use at most 64 MiB of HBM per device.

```python
import jax
import jax.numpy as jnp
from jax import lax

BLOCK = 128
SECTORS = 32
STATES = 3
TERMS_DEV = 1
BOND = 4096
TERMS = 64
SITES = 8
N_SEG = 8
N_OP = 64


def set_ends(drawn, rng, low, largest):
    longest = drawn.shape.index(max(drawn.shape))
    spots = []
    for shift in (0, 1):
        where = [jax.random.randint(jax.random.fold_in(rng, axis), (), 0, length) for axis, length in enumerate(drawn.shape)]
        where[longest] = (where[longest] + shift) % drawn.shape[longest]
        spots.append(tuple(where))
    return drawn.at[spots[0]].set(low).at[spots[1]].set(largest)


def levels(stream_key, dims, cuts, least, high):
    factor_of, own = 1.0, jax.random.fold_in(stream_key, 6)
    for dim, shards_of in cuts:
        draws = jnp.exp(jax.random.uniform(jax.random.fold_in(own, dim), (shards_of,), jnp.float32, least / len(cuts), high / len(cuts)))
        factor_of = factor_of * jnp.repeat(draws, dims[dim] // shards_of).reshape([-1 if axis == dim else 1 for axis in range(len(dims))])
    return factor_of


def centred(stream_key, shape, width, reach, shards=(), held_as=jnp.bfloat16):
    loudness = levels(stream_key, shape, shards, -0.22, 0.18) if shards else 1.0
    result = jax.random.normal(stream_key, shape, jnp.float32) * width * loudness
    return jnp.minimum(jnp.maximum(result, -reach), reach).astype(held_as)


def setup_inputs(seed: int = 0) -> dict:
    streams_of = jax.random.split(jax.random.key(seed), 7)
    site_tensor = centred(streams_of[0], (SITES, STATES, BOND, BLOCK), (BLOCK * 7 // 4) ** -0.5, 0.375, ((0, 8),))
    term_ops = centred(streams_of[1], (TERMS, BOND, BLOCK), 1.0, 6.0, ((0, 64),))
    env_rows = centred(streams_of[2], (BOND, BLOCK), 1.0, 6.0, ((0, 64),))
    term_shift = set_ends(jax.random.randint(streams_of[3], (TERMS,), -1, 2), jax.random.fold_in(streams_of[3], 1), -1, 1).astype(jnp.int32)
    keep_weight = jnp.clip(0.6 + 0.79999995 * jax.random.uniform(streams_of[4], (TERMS, STATES), jnp.float32) ** levels(streams_of[4], (TERMS, STATES), ((0, 64),), -0.2, 0.2), 0.6, 1.4)
    env_weight = centred(streams_of[5], (TERMS, STATES), (3 * TERMS) ** -0.5, 0.4375, ((0, 64),), jnp.float32)
    return {"site_tensor": site_tensor, "term_ops": term_ops, "env_rows": env_rows, "term_shift": term_shift, "keep_weight": keep_weight, "env_weight": env_weight}


def product(form, left, right):
    return jnp.einsum(form, left.astype(jnp.float32), right.astype(jnp.float32), precision=lax.Precision.HIGHEST)


def group_step(site_blocks, padded_site, ops_group, env_group, shift_group, keep_group, weight_group):
    ops_padded = jnp.pad(ops_group, ((0, 0), (2, 0), (0, 0), (0, 0)))
    env_padded = jnp.pad(env_group, ((2, 0), (0, 0), (0, 0)))

    def images_of(ops_one, term_move):
        image_list = []
        for state in range(STATES):
            right_blocks = lax.dynamic_slice_in_dim(padded_site[state], term_move + state + 2, SECTORS + 2, 0)
            image_list.append(product("lij,ljm->lim", ops_one, right_blocks).astype(jnp.bfloat16))
        return jnp.stack(image_list)

    images = jax.vmap(images_of)(ops_padded, shift_group)
    next_ops = jnp.zeros(ops_group.shape, jnp.float32)
    next_env = jnp.zeros(env_group.shape, jnp.float32)
    for state in range(STATES):
        own_blocks = site_blocks[state]
        half_env = product("rij,rjm->rim", env_padded[2 - state:2 - state + SECTORS], own_blocks).astype(jnp.bfloat16)
        next_env = next_env + product("rik,rim->rkm", own_blocks, half_env)
        own_terms = jax.vmap(lambda image_one: product("rik,rim->rkm", own_blocks, image_one[state, 2 - state:2 - state + SECTORS]))(images)
        next_ops = next_ops + keep_group[:, state][:, None, None, None] * own_terms
        partner = state - shift_group
        usable = (partner >= 0) & (partner <= 2)
        picked = jax.vmap(lambda image_one, partner_one: lax.dynamic_index_in_dim(image_one, partner_one, 0, keepdims=False))(images, jnp.clip(partner, 0, 2))
        cross_terms = jax.vmap(lambda image_one: product("rik,rim->rkm", own_blocks, image_one[2 - state:2 - state + SECTORS]))(picked)
        factors = jnp.where(usable, weight_group[:, state], 0.0)
        next_env = next_env + jnp.sum(factors[:, None, None, None] * cross_terms, axis=0)
    return next_ops.astype(jnp.bfloat16), next_env.astype(jnp.bfloat16)


def reference(site_tensor, term_ops, env_rows, term_shift, keep_weight, env_weight):
    sector_ids = jnp.arange(SECTORS, dtype=jnp.int32)
    target = sector_ids[None, :] + term_shift[:, None]
    inside = (target >= 0) & (target < SECTORS)
    start_ops = jnp.where(inside[:, :, None, None], term_ops.reshape(TERMS, SECTORS, BLOCK, BLOCK), 0.0).astype(jnp.bfloat16)
    share = BOND // N_OP
    row_owner = jnp.arange(BOND, dtype=jnp.int32) // share
    groups = jnp.arange(N_OP, dtype=jnp.int32)
    start_env = jnp.where(row_owner[None, :, None] == groups[:, None, None], env_rows[None], 0.0).astype(jnp.bfloat16)
    start_env = start_env.reshape(N_OP, SECTORS, BLOCK, BLOCK)
    ops_start = start_ops.reshape(N_OP, TERMS_DEV, SECTORS, BLOCK, BLOCK)
    shift_grouped = term_shift.reshape(N_OP, TERMS_DEV)
    keep_grouped = keep_weight.reshape(N_OP, TERMS_DEV, STATES)
    weight_grouped = env_weight.reshape(N_OP, TERMS_DEV, STATES)

    def one_segment(state_now, site_flat):
        ops_now, env_now = state_now
        site_blocks = site_flat.reshape(STATES, SECTORS, BLOCK, BLOCK)
        padded_site = jnp.pad(site_blocks, ((0, 0), (4, 4), (0, 0), (0, 0)))

        def one_group(pieces):
            ops_group, env_group, shift_group, keep_group, weight_group = pieces
            return group_step(site_blocks, padded_site, ops_group, env_group, shift_group, keep_group, weight_group)

        new_ops, new_env = lax.map(one_group, (ops_now, env_now, shift_grouped, keep_grouped, weight_grouped))
        bond = jnp.sum(new_env.astype(jnp.float32), axis=0).astype(jnp.bfloat16)
        return (new_ops, new_env), bond

    final_state, bonds = lax.scan(one_segment, (ops_start, start_env), site_tensor)
    return bonds.reshape(N_SEG, BOND, BLOCK)
```

```python
import functools

import jax
import jax.numpy as jnp
from jax import lax
from jax.experimental import pallas as pl
from jax.experimental.pallas import tpu as pltpu
from jax.sharding import Mesh, PartitionSpec as P

BLOCK = 128
OWN = 4
WINDOW = OWN + 2
STATES = 3
AXES = ("zhi", "core", "x", "zlo", "y")
BF16 = jnp.bfloat16
F32 = jnp.float32


def device_number(zhi, core, x, zlo, y):
    return (((zhi * 2 + core) * 4 + x) * 2 + zlo) * 8 + y


def all_places():
    return [
        (zhi, core, x, zlo, y)
        for zhi in range(4)
        for core in range(2)
        for x in range(4)
        for zlo in range(2)
        for y in range(8)
    ]


def to_slices():
    return [
        (device_number(*place), device_number(place[4] // 2, place[4] % 2, place[2], place[3], place[0] * 2 + place[1]))
        for place in all_places()
    ]


def rows_to_slices(back, halo=False):
    pairs = []
    for zhi, core, x, zlo, y in all_places():
        if not back and (zhi or core):
            continue
        if halo and (y < 4 or 2 * x + zlo == 7):
            continue
        outer = device_number(zhi, core, x, zlo, y)
        inner = device_number(zhi, core, y // 2, y % 2, 2 * x + zlo + (1 if halo else 0))
        pairs.append((inner, outer) if back else (outer, inner))
    return pairs


def site_piece(site_blocks, slice_at, half):
    sectors = site_blocks.shape[1]
    first = OWN * slice_at - 1 + 3 * half
    taken = lax.dynamic_slice_in_dim(site_blocks, jnp.clip(first, 0, sectors - 3), 3, 1)
    zero = jnp.zeros_like(taken[:, :1])
    low = jnp.concatenate([zero, taken[:, :2]], 1)
    high = jnp.concatenate([taken[:, 1:], zero], 1)
    return jnp.where(first < 0, low, jnp.where(first > sectors - 3, high, taken))


def ops_piece(ops_blocks, shift, slice_at):
    sectors = ops_blocks.shape[0]
    first = OWN * slice_at - 2
    taken = lax.dynamic_slice_in_dim(ops_blocks, jnp.maximum(first, 0), WINDOW, 0)
    low = jnp.concatenate([jnp.zeros_like(taken[:2]), taken[:OWN]], 0)
    taken = jnp.where(first < 0, low, taken)
    target = first + jnp.arange(WINDOW, dtype=jnp.int32) + shift
    inside = (target >= 0) & (target < sectors)
    return jnp.where(inside[:, None, None], taken, jnp.zeros((), BF16))


def phase_kernel(sites, steps, n_in, sources, targets, with_ops, *refs):
    whole, part, mine, other = refs[:4]
    ins = refs[4 : 4 + n_in]
    outs = refs[4 + n_in : -2]
    site_at, sems = refs[-2:]
    core = whole[0]
    shift = whole[1]

    def copies(slot, site, source):
        return [
            pltpu.make_async_copy(
                source.at[(site // 2) * 2 + half],
                site_at.at[slot, :, pl.ds(3 * half, 3)],
                sems.at[slot, half],
            )
            for half in range(2)
        ]

    for slot, site in enumerate(sites):
        @pl.when(core == site % 2)
        def _():
            for copy in copies(slot, site, mine):
                copy.start()

        @pl.when(core != site % 2)
        def _():
            for copy in copies(slot, site, other):
                copy.start()

    done_sites = set()
    state = {}

    def get(site, sector):
        if (site, sector) in state:
            return state[site, sector]
        where, index = sources[site, sector]
        return ins[where][index]

    for site, first in steps:
        slot = sites.index(site)
        if site not in done_sites:
            done_sites.add(site)
            for copy in copies(slot, site, mine):
                copy.wait()
        for sector in (first, first + 1):
            total = None
            for s in range(STATES):
                block = get(site, sector - s)
                ops, env = block[:, :BLOCK], block[:, BLOCK:]
                left = site_at[slot, s, sector + 1]
                cross = site_at[slot, jnp.clip(s - shift, 0, 2), sector + 1]
                half_env = jnp.dot(env, left, preferred_element_type=F32)
                if with_ops(site):
                    right = site_at[slot, s, sector + 1 + shift]
                    both = jnp.dot(ops, jnp.concatenate([right, cross], 1), preferred_element_type=F32)
                    image = jnp.concatenate(
                        [part[s] * both[:, :BLOCK], half_env + part[3 + s] * both[:, BLOCK:]], 1
                    )
                else:
                    image = half_env + part[3 + s] * jnp.dot(ops, cross, preferred_element_type=F32)
                product = lax.dot_general(
                    left, image.astype(BF16), (((0,), (0,)), ((), ())), preferred_element_type=F32
                )
                total = product if total is None else total + product
            total = total.astype(BF16)
            state[site + 1, sector] = total
            for which, index in targets[site + 1, sector]:
                outs[which][index] = total


def run_phase(sites, steps, ins, sources, outs, targets, with_ops, whole, part, mine, other):
    blocks = 2 * len(steps) * (15 if with_ops(sites[0]) else 9)
    return pl.pallas_call(
        functools.partial(phase_kernel, sites, steps, len(ins), sources, targets, with_ops),
        out_shape=[jax.ShapeDtypeStruct(shape, BF16) for shape in outs],
        in_specs=[pl.BlockSpec(memory_space=pltpu.SMEM)] * 2
        + [pl.BlockSpec(memory_space=pl.ANY)] * 2
        + [pl.BlockSpec(memory_space=pltpu.VMEM)] * len(ins),
        out_specs=[pl.BlockSpec(memory_space=pltpu.VMEM)] * len(outs),
        scratch_shapes=[
            pltpu.VMEM((len(sites), STATES, WINDOW, BLOCK, BLOCK), BF16),
            pltpu.SemaphoreType.DMA((len(sites), 2)),
        ],
        compiler_params=pltpu.CompilerParams(vmem_limit_bytes=32 * 1024 * 1024),
        cost_estimate=pl.CostEstimate(flops=blocks * 2 * BLOCK**3, bytes_accessed=4 << 20, transcendentals=0),
    )(whole, part, mine, other, *ins)


def body(site_tensor, term_ops, env_rows, term_shift, keep_weight, env_weight):
    sectors = site_tensor.shape[2] // BLOCK
    core = lax.axis_index("core")
    seg = lax.axis_index("zhi") * 2 + core
    at_x, at_zlo, at_y = (lax.axis_index(name) for name in ("x", "zlo", "y"))

    site_blocks = site_tensor[0].reshape(STATES, sectors, BLOCK, BLOCK)
    mine = lax.all_gather(site_piece(site_blocks, at_y, at_zlo), ("zhi", "zlo"))
    other = lax.ppermute(mine, "core", [(0, 1), (1, 0)])

    own_ops = ops_piece(term_ops[0].reshape(sectors, BLOCK, BLOCK), term_shift[0], seg)
    ops_now = lax.ppermute(own_ops, AXES, to_slices())
    figures = jnp.concatenate([keep_weight[0], env_weight[0], term_shift.astype(F32), jnp.zeros((1,), F32)])
    figures = lax.ppermute(figures, AXES, to_slices())
    shift = figures[6].astype(jnp.int32)
    partner = jnp.arange(STATES, dtype=jnp.int32) - shift
    factors = jnp.where((partner >= 0) & (partner <= 2), figures[3:6], 0.0)
    part = jnp.concatenate([figures[:3], factors])
    whole = jnp.stack([core.astype(jnp.int32), shift])

    piece = lax.ppermute(env_rows, AXES, rows_to_slices(False))
    halo = lax.ppermute(env_rows, AXES, rows_to_slices(False, True))
    env_now = jnp.zeros((WINDOW * BLOCK, BLOCK), BF16)
    spot = at_x * BLOCK + at_zlo * (BLOCK // 2)
    env_now = lax.dynamic_update_slice_in_dim(env_now, halo, jnp.maximum(spot - 2 * BLOCK, 0), 0)
    env_now = lax.dynamic_update_slice_in_dim(env_now, piece, spot + 2 * BLOCK, 0)
    window = jnp.concatenate([ops_now, env_now.reshape(WINDOW, BLOCK, BLOCK)], 2)

    wide = (BLOCK, 2 * BLOCK)
    onward = [(i, i + 1) for i in range(7)]

    def always(site):
        return True

    def before_last(site):
        return site < 7

    targets = {}
    for sector in range(OWN):
        targets[1, sector] = [(0, sector)] + ([(2, (0, sector - 2))] if sector >= 2 else [])
    for sector in (2, 3):
        targets[2, sector] = [(1, sector - 2), (2, (1, sector - 2))]
    sources = {(0, sector): (0, sector + 2) for sector in range(-2, OWN)}
    full, upper, tails = run_phase(
        [0, 1],
        [(0, 2), (0, 0), (1, 2)],
        [window],
        sources,
        [(OWN,) + wide, (2,) + wide, (2, 2) + wide],
        targets,
        always,
        whole,
        part,
        mine,
        other,
    )
    bonds = [full[:, :, BLOCK:]]
    for site in (1, 3, 5):
        tails = lax.ppermute(tails, "y", onward)
        last = site == 5
        sources = {}
        for sector in (-2, -1):
            sources[site, sector] = (2, (0, sector + 2))
            sources[site + 1, sector] = (2, (1, sector + 2))
        for sector in range(OWN):
            sources[site, sector] = (0, sector)
        for sector in (2, 3):
            sources[site + 1, sector] = (1, sector - 2)
        targets = {}
        for sector in (0, 1):
            targets[site + 1, sector] = [(0, sector)]
        for sector in range(OWN):
            targets[site + 2, sector] = [(1, sector)] + ([(3, (0, sector - 2))] if sector >= 2 else [])
        for sector in (2, 3):
            targets[site + 3, sector] = [(2, sector - 2)] + ([] if last else [(3, (1, sector - 2))])
        old_upper = upper
        narrow = (BLOCK, BLOCK)
        lower, full, upper, tails = run_phase(
            [site, site + 1, site + 2],
            [(site, 0), (site + 1, 2), (site + 1, 0), (site + 2, 2)],
            [full, upper, tails],
            sources,
            [(2,) + wide, (OWN,) + wide, (2,) + (narrow if last else wide), (1 if last else 2, 2) + wide],
            targets,
            before_last,
            whole,
            part,
            mine,
            other,
        )
        bonds += [lower[:, :, BLOCK:], old_upper[:, :, BLOCK:], full[:, :, BLOCK:]]
    tails = lax.ppermute(tails, "y", onward)
    sources = {(7, sector): (1, (0, sector + 2)) for sector in (-2, -1)}
    sources.update({(7, sector): (0, sector) for sector in range(2)})
    (lower,) = run_phase(
        [7],
        [(7, 0)],
        [full, tails],
        sources,
        [(2, BLOCK, BLOCK)],
        {(8, sector): [(0, sector)] for sector in (0, 1)},
        before_last,
        whole,
        part,
        mine,
        other,
    )
    bonds += [lower, upper]

    partial = jnp.concatenate(bonds, 0).reshape(4, 2, 8, BLOCK // 2, BLOCK).transpose(1, 0, 2, 3, 4)
    over = lax.all_to_all(partial, "core", 0, 0)
    summed = over.astype(F32).sum(0).astype(BF16)
    summed = summed.transpose(1, 0, 2, 3)
    over = lax.all_to_all(summed, ("x", "zlo"), 0, 0)
    summed = over.astype(F32).sum(0).astype(BF16)
    over = lax.all_to_all(summed, "zhi", 0, 0)
    summed = over.astype(F32).sum(0).astype(BF16)
    return lax.ppermute(summed, AXES, rows_to_slices(True))[None]


def solution(mesh):
    parts = Mesh(mesh.devices.reshape(4, 2, 4, 2, 8), AXES)
    seg, op = ("zhi", "core"), ("x", "zlo", "y")
    placed = (P(seg, None, None, None), P(op, None, None), P(op, None), P(op), P(op, None), P(op, None))
    return jax.shard_map(body, mesh=parts, in_specs=placed, out_specs=P(seg, op, None), check_vma=False)
```

```python
import functools

import jax
import jax.numpy as jnp
from jax import lax
from jax.experimental import pallas as pl
from jax.experimental.pallas import tpu as pltpu
from jax.sharding import Mesh, PartitionSpec as P

BLOCK = 128
OWN = 4
WINDOW = OWN + 2
STATES = 3
AXES = ("zhi", "core", "x", "zlo", "y")
BF16 = jnp.bfloat16
F32 = jnp.float32


def device_number(zhi, core, x, zlo, y):
    return (((zhi * 2 + core) * 4 + x) * 2 + zlo) * 8 + y


def all_places():
    return [
        (zhi, core, x, zlo, y)
        for zhi in range(4)
        for core in range(2)
        for x in range(4)
        for zlo in range(2)
        for y in range(8)
    ]


def to_slices():
    return [
        (device_number(*place), device_number(place[4] // 2, place[4] % 2, place[2], place[3], place[0] * 2 + place[1]))
        for place in all_places()
    ]


def rows_to_slices(back, halo=False):
    pairs = []
    for zhi, core, x, zlo, y in all_places():
        if not back and (zhi or core):
            continue
        if halo and (y < 4 or 2 * x + zlo == 7):
            continue
        outer = device_number(zhi, core, x, zlo, y)
        inner = device_number(zhi, core, y // 2, y % 2, 2 * x + zlo + (1 if halo else 0))
        pairs.append((inner, outer) if back else (outer, inner))
    return pairs


def site_start(sectors, slice_at, half):
    return jnp.clip(OWN * slice_at - 1 + 3 * half, 0, sectors - 3)


def ops_piece(ops_blocks, shift, slice_at):
    sectors = ops_blocks.shape[0]
    first = OWN * slice_at - 2
    taken = lax.dynamic_slice_in_dim(ops_blocks, jnp.maximum(first, 0), WINDOW, 0)
    low = jnp.concatenate([jnp.zeros_like(taken[:2]), taken[:OWN]], 0)
    taken = jnp.where(first < 0, low, taken)
    target = first + jnp.arange(WINDOW, dtype=jnp.int32) + shift
    inside = (target >= 0) & (target < sectors)
    return jnp.where(inside[:, None, None], taken, jnp.zeros((), BF16))


def phase_kernel(sites, steps, n_in, sources, targets, with_ops, *refs):
    whole, part, mine, other = refs[:4]
    ins = refs[4 : 4 + n_in]
    outs = refs[4 + n_in : -2]
    site_at, sems = refs[-2:]
    core = whole[0]
    shift = whole[1]

    def copies(slot, site, source):
        return [
            pltpu.make_async_copy(
                source.at[(site // 2) * 2 + half],
                site_at.at[slot, :, pl.ds(whole[2 + half], 3)],
                sems.at[slot, half],
            )
            for half in range(2)
        ]

    @pl.when(whole[2] != 0)
    def _():
        site_at[:, :, 0] = jnp.zeros((len(sites), STATES, BLOCK, BLOCK), BF16)

    @pl.when(whole[3] != 3)
    def _():
        site_at[:, :, WINDOW - 1] = jnp.zeros((len(sites), STATES, BLOCK, BLOCK), BF16)

    for slot, site in enumerate(sites):
        @pl.when(core == site % 2)
        def _():
            for copy in copies(slot, site, mine):
                copy.start()

        @pl.when(core != site % 2)
        def _():
            for copy in copies(slot, site, other):
                copy.start()

    done_sites = set()
    state = {}

    def get(site, sector):
        if (site, sector) in state:
            return state[site, sector]
        where, index = sources[site, sector]
        return ins[where][index]

    for site, first in steps:
        slot = sites.index(site)
        if site not in done_sites:
            done_sites.add(site)
            for copy in copies(slot, site, mine):
                copy.wait()
        for sector in (first, first + 1):
            total = None
            for s in range(STATES):
                block = get(site, sector - s)
                ops, env = block[:, :BLOCK], block[:, BLOCK:]
                left = site_at[slot, s, sector + 1]
                cross = site_at[slot, jnp.clip(s - shift, 0, 2), sector + 1]
                half_env = jnp.dot(env, left, preferred_element_type=F32)
                if with_ops(site):
                    right = site_at[slot, s, sector + 1 + shift]
                    both = jnp.dot(ops, jnp.concatenate([right, cross], 1), preferred_element_type=F32)
                    image = jnp.concatenate(
                        [part[s] * both[:, :BLOCK], half_env + part[3 + s] * both[:, BLOCK:]], 1
                    )
                else:
                    image = half_env + part[3 + s] * jnp.dot(ops, cross, preferred_element_type=F32)
                product = lax.dot_general(
                    left, image.astype(BF16), (((0,), (0,)), ((), ())), preferred_element_type=F32
                )
                total = product if total is None else total + product
            total = total.astype(BF16)
            state[site + 1, sector] = total
            for which, index in targets[site + 1, sector]:
                outs[which][index] = total


def run_phase(sites, steps, ins, sources, outs, targets, with_ops, whole, part, mine, other):
    blocks = 2 * len(steps) * (15 if with_ops(sites[0]) else 9)
    return pl.pallas_call(
        functools.partial(phase_kernel, sites, steps, len(ins), sources, targets, with_ops),
        out_shape=[jax.ShapeDtypeStruct(shape, BF16) for shape in outs],
        in_specs=[pl.BlockSpec(memory_space=pltpu.SMEM)] * 2
        + [pl.BlockSpec(memory_space=pl.ANY)] * 2
        + [pl.BlockSpec(memory_space=pltpu.VMEM)] * len(ins),
        out_specs=[pl.BlockSpec(memory_space=pltpu.VMEM)] * len(outs),
        scratch_shapes=[
            pltpu.VMEM((len(sites), STATES, WINDOW, BLOCK, BLOCK), BF16),
            pltpu.SemaphoreType.DMA((len(sites), 2)),
        ],
        compiler_params=pltpu.CompilerParams(vmem_limit_bytes=32 * 1024 * 1024),
        cost_estimate=pl.CostEstimate(flops=blocks * 2 * BLOCK**3, bytes_accessed=4 << 20, transcendentals=0),
    )(whole, part, mine, other, *ins)


def body(site_tensor, term_ops, env_rows, term_shift, keep_weight, env_weight):
    sectors = site_tensor.shape[2] // BLOCK
    core = lax.axis_index("core")
    seg = lax.axis_index("zhi") * 2 + core
    at_x, at_zlo, at_y = (lax.axis_index(name) for name in ("x", "zlo", "y"))

    site_blocks = site_tensor[0].reshape(STATES, sectors, BLOCK, BLOCK)
    piece = lax.dynamic_slice_in_dim(site_blocks, site_start(sectors, at_y, at_zlo), 3, 1)
    mine = lax.all_gather(piece, ("zhi", "zlo"))
    spots = [site_start(sectors, at_y, half) - (OWN * at_y - 1) for half in range(2)]

    own_ops = ops_piece(term_ops[0].reshape(sectors, BLOCK, BLOCK), term_shift[0], seg)
    ops_now = lax.ppermute(own_ops, AXES, to_slices())
    figures = jnp.concatenate([keep_weight[0], env_weight[0], term_shift.astype(F32), jnp.zeros((1,), F32)])
    figures = lax.ppermute(figures, AXES, to_slices())
    shift = figures[6].astype(jnp.int32)
    partner = jnp.arange(STATES, dtype=jnp.int32) - shift
    factors = jnp.where((partner >= 0) & (partner <= 2), figures[3:6], 0.0)
    part = jnp.concatenate([figures[:3], factors])
    whole = jnp.stack([core, shift] + spots).astype(jnp.int32)

    piece = lax.ppermute(env_rows, AXES, rows_to_slices(False))
    halo = lax.ppermute(env_rows, AXES, rows_to_slices(False, True))
    env_now = jnp.zeros((WINDOW * BLOCK, BLOCK), BF16)
    spot = at_x * BLOCK + at_zlo * (BLOCK // 2)
    env_now = lax.dynamic_update_slice_in_dim(env_now, halo, jnp.maximum(spot - 2 * BLOCK, 0), 0)
    env_now = lax.dynamic_update_slice_in_dim(env_now, piece, spot + 2 * BLOCK, 0)
    window = jnp.concatenate([ops_now, env_now.reshape(WINDOW, BLOCK, BLOCK)], 2)

    mine, window, whole, part = lax.optimization_barrier((mine, window, whole, part))
    other = lax.ppermute(mine, "core", [(0, 1), (1, 0)])

    wide = (BLOCK, 2 * BLOCK)
    onward = [(i, i + 1) for i in range(7)]

    def always(site):
        return True

    def before_last(site):
        return site < 7

    targets = {}
    for sector in range(OWN):
        targets[1, sector] = [(0, sector)] + ([(2, (0, sector - 2))] if sector >= 2 else [])
    for sector in (2, 3):
        targets[2, sector] = [(1, sector - 2), (2, (1, sector - 2))]
    sources = {(0, sector): (0, sector + 2) for sector in range(-2, OWN)}
    full, upper, tails = run_phase(
        [0, 1],
        [(0, 2), (0, 0), (1, 2)],
        [window],
        sources,
        [(OWN,) + wide, (2,) + wide, (2, 2) + wide],
        targets,
        always,
        whole,
        part,
        mine,
        other,
    )
    bonds = [full[:, :, BLOCK:]]
    for site in (1, 3, 5):
        tails = lax.ppermute(tails, "y", onward)
        last = site == 5
        sources = {}
        for sector in (-2, -1):
            sources[site, sector] = (2, (0, sector + 2))
            sources[site + 1, sector] = (2, (1, sector + 2))
        for sector in range(OWN):
            sources[site, sector] = (0, sector)
        for sector in (2, 3):
            sources[site + 1, sector] = (1, sector - 2)
        targets = {}
        for sector in (0, 1):
            targets[site + 1, sector] = [(0, sector)]
        for sector in range(OWN):
            targets[site + 2, sector] = [(1, sector)] + ([(3, (0, sector - 2))] if sector >= 2 else [])
        for sector in (2, 3):
            targets[site + 3, sector] = [(2, sector - 2)] + ([] if last else [(3, (1, sector - 2))])
        old_upper = upper
        narrow = (BLOCK, BLOCK)
        lower, full, upper, tails = run_phase(
            [site, site + 1, site + 2],
            [(site, 0), (site + 1, 2), (site + 1, 0), (site + 2, 2)],
            [full, upper, tails],
            sources,
            [(2,) + wide, (OWN,) + wide, (2,) + (narrow if last else wide), (1 if last else 2, 2) + wide],
            targets,
            before_last,
            whole,
            part,
            mine,
            other,
        )
        bonds += [lower[:, :, BLOCK:], old_upper[:, :, BLOCK:], full[:, :, BLOCK:]]
    tails = lax.ppermute(tails, "y", onward)
    sources = {(7, sector): (1, (0, sector + 2)) for sector in (-2, -1)}
    sources.update({(7, sector): (0, sector) for sector in range(2)})
    (lower,) = run_phase(
        [7],
        [(7, 0)],
        [full, tails],
        sources,
        [(2, BLOCK, BLOCK)],
        {(8, sector): [(0, sector)] for sector in (0, 1)},
        before_last,
        whole,
        part,
        mine,
        other,
    )
    bonds += [lower, upper]

    partial = jnp.concatenate(bonds, 0).reshape(4, 2, 8, BLOCK // 2, BLOCK).transpose(1, 0, 2, 3, 4)
    over = lax.all_to_all(partial, "core", 0, 0)
    summed = over.astype(F32).sum(0).astype(BF16)
    summed = summed.reshape(32, BLOCK // 2, BLOCK)
    over = lax.all_to_all(summed, ("zhi", "x", "zlo"), 0, 0)
    summed = over.astype(F32).sum(0).astype(BF16)
    return lax.ppermute(summed, AXES, rows_to_slices(True))[None]


def solution(mesh):
    parts = Mesh(mesh.devices.reshape(4, 2, 4, 2, 8), AXES)
    seg, op = ("zhi", "core"), ("x", "zlo", "y")
    placed = (P(seg, None, None, None), P(op, None, None), P(op, None), P(op), P(op, None), P(op, None))
    return jax.shard_map(body, mesh=parts, in_specs=placed, out_specs=P(seg, op, None), check_vma=False)
```

```python
import functools
import itertools

import jax
import jax.numpy as jnp
from jax import lax
from jax.experimental import pallas as pl
from jax.experimental.pallas import tpu as pltpu
from jax.sharding import Mesh, PartitionSpec as P

BLOCK = 128
OWN = 4
WINDOW = OWN + 2
STATES = 3
AXES = ("zhi", "core", "x", "zlo", "yl", "y0")
BF16 = jnp.bfloat16
F32 = jnp.float32


def device_number(zhi, core, x, zlo, yl, y0):
    return ((((zhi * 2 + core) * 4 + x) * 2 + zlo) * 4 + yl) * 2 + y0


def all_places():
    return itertools.product(range(4), range(2), range(4), range(2), range(4), range(2))


def to_groups():
    return [
        (device_number(zhi, core, x, zlo, yl, y0), device_number(x, y0, zhi, zlo, yl, core))
        for zhi, core, x, zlo, yl, y0 in all_places()
    ]


def rows_to_groups(halo):
    pairs = []
    for zhi, core, x, zlo, yl, y0 in all_places():
        group = 2 * x + zlo + halo
        if zhi == core == 0 and group < 8 and not (halo and yl < 2):
            target = device_number(0, 0, group // 2, y0, yl, group % 2)
            pairs.append((device_number(0, 0, x, zlo, yl, y0), target))
    return pairs


def site_start(sectors, slice_at, half):
    return jnp.clip(OWN * slice_at - 1 + 3 * half, 0, sectors - 3)


def ops_piece(ops_blocks, shift, slice_at):
    sectors = ops_blocks.shape[0]
    first = OWN * slice_at - 2
    taken = lax.dynamic_slice_in_dim(ops_blocks, jnp.maximum(first, 0), WINDOW, 0)
    low = jnp.concatenate([jnp.zeros_like(taken[:2]), taken[:OWN]], 0)
    taken = jnp.where(first < 0, low, taken)
    target = first + jnp.arange(WINDOW, dtype=jnp.int32) + shift
    inside = (target >= 0) & (target < sectors)
    return jnp.where(inside[:, None, None], taken, jnp.zeros((), BF16))


def phase_kernel(sites, steps, n_in, sources, targets, with_ops, *refs):
    whole, part, mine, other = refs[:4]
    ins = refs[4 : 4 + n_in]
    outs = refs[4 + n_in : -2]
    site_at, sems = refs[-2:]
    core = whole[0]
    shift = whole[1]

    def copies(slot, site, source):
        return [
            pltpu.make_async_copy(
                source.at[(site // 2) * 2 + half],
                site_at.at[slot, :, pl.ds(whole[2 + half], 3)],
                sems.at[slot, half],
            )
            for half in range(2)
        ]

    @pl.when(whole[2] != 0)
    def _():
        site_at[:, :, 0] = jnp.zeros((len(sites), STATES, BLOCK, BLOCK), BF16)

    @pl.when(whole[3] != 3)
    def _():
        site_at[:, :, WINDOW - 1] = jnp.zeros((len(sites), STATES, BLOCK, BLOCK), BF16)

    for slot, site in enumerate(sites):
        @pl.when(core == site % 2)
        def _():
            for copy in copies(slot, site, mine):
                copy.start()

        @pl.when(core != site % 2)
        def _():
            for copy in copies(slot, site, other):
                copy.start()

    done_sites = set()
    state = {}

    def get(site, sector):
        if (site, sector) in state:
            return state[site, sector]
        where, index = sources[site, sector]
        return ins[where][index]

    for site, first in steps:
        slot = sites.index(site)
        if site not in done_sites:
            done_sites.add(site)
            for copy in copies(slot, site, mine):
                copy.wait()
        for sector in (first, first + 1):
            total = None
            for s in range(STATES):
                block = get(site, sector - s)
                ops, env = block[:, :BLOCK], block[:, BLOCK:]
                left = site_at[slot, s, sector + 1]
                cross = site_at[slot, jnp.clip(s - shift, 0, 2), sector + 1]
                half_env = jnp.dot(env, left, preferred_element_type=F32)
                if with_ops(site):
                    right = site_at[slot, s, sector + 1 + shift]
                    both = jnp.dot(ops, jnp.concatenate([right, cross], 1), preferred_element_type=F32)
                    image = jnp.concatenate(
                        [part[s] * both[:, :BLOCK], half_env + part[3 + s] * both[:, BLOCK:]], 1
                    )
                else:
                    image = half_env + part[3 + s] * jnp.dot(ops, cross, preferred_element_type=F32)
                product = lax.dot_general(
                    left, image.astype(BF16), (((0,), (0,)), ((), ())), preferred_element_type=F32
                )
                total = product if total is None else total + product
            total = total.astype(BF16)
            state[site + 1, sector] = total
            for which, index in targets[site + 1, sector]:
                outs[which][index] = total


def run_phase(sites, steps, ins, sources, outs, targets, with_ops, whole, part, mine, other):
    blocks = 2 * len(steps) * (15 if with_ops(sites[0]) else 9)
    return pl.pallas_call(
        functools.partial(phase_kernel, sites, steps, len(ins), sources, targets, with_ops),
        out_shape=[jax.ShapeDtypeStruct(shape, BF16) for shape in outs],
        in_specs=[pl.BlockSpec(memory_space=pltpu.SMEM)] * 2
        + [pl.BlockSpec(memory_space=pl.ANY)] * 2
        + [pl.BlockSpec(memory_space=pltpu.VMEM)] * len(ins),
        out_specs=[pl.BlockSpec(memory_space=pltpu.VMEM)] * len(outs),
        scratch_shapes=[
            pltpu.VMEM((len(sites), STATES, WINDOW, BLOCK, BLOCK), BF16),
            pltpu.SemaphoreType.DMA((len(sites), 2)),
        ],
        compiler_params=pltpu.CompilerParams(vmem_limit_bytes=32 * 1024 * 1024),
        cost_estimate=pl.CostEstimate(flops=blocks * 2 * BLOCK**3, bytes_accessed=4 << 20, transcendentals=0),
    )(whole, part, mine, other, *ins)


def take_piece(start, site, piece, taken, sems):
    rows = 3 * BLOCK
    first = pl.multiple_of(start[0] * BLOCK, BLOCK)
    inward = [
        pltpu.make_async_copy(site.at[0, s, pl.ds(first, rows)], taken.at[s], sems.at[0, s]) for s in range(STATES)
    ]
    outward = [pltpu.make_async_copy(taken.at[s], piece.at[s], sems.at[1, s]) for s in range(STATES)]
    for copy in inward:
        copy.start()
    for before, after in zip(inward, outward):
        before.wait()
        after.start()
    for copy in outward:
        copy.wait()


def add_cores(over, summed):
    for site in range(4):
        summed[site] = (over[0, site].astype(F32) + over[1, site].astype(F32)).astype(BF16)


def add_columns(place, over, summed):
    total = over[0].astype(F32)
    for source in range(1, 16):
        total += over[source].astype(F32)
    total = total.astype(BF16)
    for zlo in range(2):
        summed[zlo] = jnp.where(place[0] == zlo, total, jnp.zeros_like(total))


def add_up(kernel, ins, out):
    spaces = [pltpu.SMEM if array.ndim == 1 else pltpu.VMEM for array in ins]
    return pl.pallas_call(
        kernel,
        out_shape=jax.ShapeDtypeStruct(out, BF16),
        in_specs=[pl.BlockSpec(memory_space=space) for space in spaces],
        out_specs=pl.BlockSpec(memory_space=pltpu.VMEM),
        compiler_params=pltpu.CompilerParams(vmem_limit_bytes=16 << 20),
        cost_estimate=pl.CostEstimate(flops=1 << 19, bytes_accessed=2 << 20, transcendentals=0),
    )(*ins)


def body(site_tensor, term_ops, env_rows, term_shift, keep_weight, env_weight):
    sectors = site_tensor.shape[2] // BLOCK
    core = lax.axis_index("core")
    seg = lax.axis_index("zhi") * 2 + core
    at_zlo, at_yl, at_y0 = (lax.axis_index(name) for name in ("zlo", "yl", "y0"))
    group = lax.axis_index("x") * 2 + at_y0

    start = site_start(sectors, group, at_zlo).astype(jnp.int32).reshape(1)
    piece = pl.pallas_call(
        take_piece,
        out_shape=jax.ShapeDtypeStruct((STATES, 3 * BLOCK, BLOCK), BF16),
        in_specs=[pl.BlockSpec(memory_space=pltpu.SMEM), pl.BlockSpec(memory_space=pltpu.HBM)],
        out_specs=pl.BlockSpec(memory_space=pltpu.HBM),
        scratch_shapes=[pltpu.VMEM((STATES, 3 * BLOCK, BLOCK), BF16), pltpu.SemaphoreType.DMA((2, STATES))],
        compiler_params=pltpu.CompilerParams(vmem_limit_bytes=60 << 20),
        cost_estimate=pl.CostEstimate(flops=0, bytes_accessed=600_000, transcendentals=0),
    )(start, site_tensor).reshape(STATES, 3, BLOCK, BLOCK)
    mine = lax.all_gather(piece, ("zhi", "zlo"))
    spots = [site_start(sectors, group, half) - (OWN * group - 1) for half in range(2)]

    own_ops = ops_piece(term_ops[0].reshape(sectors, BLOCK, BLOCK), term_shift[0], seg)
    ops_now = lax.ppermute(own_ops, AXES, to_groups())
    figures = jnp.concatenate([keep_weight[0], env_weight[0], term_shift.astype(F32), jnp.zeros((1,), F32)])
    figures = lax.ppermute(figures, AXES, to_groups())
    shift = figures[6].astype(jnp.int32)
    partner = jnp.arange(STATES, dtype=jnp.int32) - shift
    factors = jnp.where((partner >= 0) & (partner <= 2), figures[3:6], 0.0)
    part = jnp.concatenate([figures[:3], factors])
    whole = jnp.stack([core, shift] + spots).astype(jnp.int32)

    piece = lax.ppermute(env_rows, AXES, rows_to_groups(0))
    halo = lax.ppermute(env_rows, AXES, rows_to_groups(1))
    env_now = jnp.zeros((WINDOW * BLOCK, BLOCK), BF16)
    spot = at_yl * BLOCK + at_zlo * (BLOCK // 2)
    env_now = lax.dynamic_update_slice_in_dim(env_now, halo, jnp.maximum(spot - 2 * BLOCK, 0), 0)
    env_now = lax.dynamic_update_slice_in_dim(env_now, piece, spot + 2 * BLOCK, 0)
    window = jnp.concatenate([ops_now, env_now.reshape(WINDOW, BLOCK, BLOCK)], 2)

    mine, window, whole, part = lax.optimization_barrier((mine, window, whole, part))
    other = lax.ppermute(mine, "core", [(0, 1), (1, 0)])

    wide = (BLOCK, 2 * BLOCK)
    onward = [(i, i + 1) for i in range(7)]

    def always(site):
        return True

    def before_last(site):
        return site < 7

    targets = {}
    for sector in range(OWN):
        targets[1, sector] = [(0, sector)] + ([(2, (0, sector - 2))] if sector >= 2 else [])
    for sector in (2, 3):
        targets[2, sector] = [(1, sector - 2), (2, (1, sector - 2))]
    sources = {(0, sector): (0, sector + 2) for sector in range(-2, OWN)}
    full, upper, tails = run_phase(
        [0, 1],
        [(0, 2), (0, 0), (1, 2)],
        [window],
        sources,
        [(OWN,) + wide, (2,) + wide, (2, 2) + wide],
        targets,
        always,
        whole,
        part,
        mine,
        other,
    )
    bonds = [full[:, :, BLOCK:]]
    for site in (1, 3, 5):
        tails = lax.ppermute(tails, ("x", "y0"), onward)
        last = site == 5
        sources = {}
        for sector in (-2, -1):
            sources[site, sector] = (2, (0, sector + 2))
            sources[site + 1, sector] = (2, (1, sector + 2))
        for sector in range(OWN):
            sources[site, sector] = (0, sector)
        for sector in (2, 3):
            sources[site + 1, sector] = (1, sector - 2)
        targets = {}
        for sector in (0, 1):
            targets[site + 1, sector] = [(0, sector)]
        for sector in range(OWN):
            targets[site + 2, sector] = [(1, sector)] + ([(3, (0, sector - 2))] if sector >= 2 else [])
        for sector in (2, 3):
            targets[site + 3, sector] = [(2, sector - 2)] + ([] if last else [(3, (1, sector - 2))])
        old_upper = upper
        narrow = (BLOCK, BLOCK)
        lower, full, upper, tails = run_phase(
            [site, site + 1, site + 2],
            [(site, 0), (site + 1, 2), (site + 1, 0), (site + 2, 2)],
            [full, upper, tails],
            sources,
            [(2,) + wide, (OWN,) + wide, (2,) + (narrow if last else wide), (1 if last else 2, 2) + wide],
            targets,
            before_last,
            whole,
            part,
            mine,
            other,
        )
        bonds += [lower[:, :, BLOCK:], old_upper[:, :, BLOCK:], full[:, :, BLOCK:]]
    tails = lax.ppermute(tails, ("x", "y0"), onward)
    sources = {(7, sector): (1, (0, sector + 2)) for sector in (-2, -1)}
    sources.update({(7, sector): (0, sector) for sector in range(2)})
    (lower,) = run_phase(
        [7],
        [(7, 0)],
        [full, tails],
        sources,
        [(2, BLOCK, BLOCK)],
        {(8, sector): [(0, sector)] for sector in (0, 1)},
        before_last,
        whole,
        part,
        mine,
        other,
    )
    bonds += [lower, upper]

    partial = jnp.concatenate(bonds, 0).reshape(4, 2, 8, BLOCK // 2, BLOCK).transpose(1, 0, 2, 3, 4)
    over = lax.all_to_all(partial, "core", 0, 0)
    summed = add_up(add_cores, [over], (4, 8, BLOCK // 2, BLOCK)).reshape(16, 2, BLOCK // 2, BLOCK)
    over = lax.all_to_all(summed, ("zhi", "yl"), 0, 0)
    place = at_y0.astype(jnp.int32).reshape(1)
    summed = add_up(add_columns, [place, over], (2, 2, BLOCK // 2, BLOCK)).reshape(4, BLOCK // 2, BLOCK)
    over = lax.all_to_all(summed, ("zlo", "y0"), 0, 0)
    return over.astype(F32).sum(0).astype(BF16)[None]


def solution(mesh):
    parts = Mesh(mesh.devices.reshape(4, 2, 4, 2, 4, 2), AXES)
    seg, op = ("zhi", "core"), ("x", "zlo", "yl", "y0")
    placed = (P(seg, None, None, None), P(op, None, None), P(op, None), P(op), P(op, None), P(op, None))
    return jax.shard_map(body, mesh=parts, in_specs=placed, out_specs=P(seg, op, None), check_vma=False)
```

```python
import functools
import itertools

import jax
import jax.numpy as jnp
from jax import lax
from jax.experimental import pallas as pl
from jax.experimental.pallas import tpu as pltpu
from jax.sharding import Mesh, PartitionSpec as P

BLOCK = 128
OWN = 4
HALF = 4
WINDOW = 2 * HALF
BEFORE = 3
STATES = 3
AXES = ("zhi", "core", "x", "zlo", "yl", "y0")
BF16 = jnp.bfloat16
F32 = jnp.float32


def device_number(zhi, core, x, zlo, yl, y0):
    return ((((zhi * 2 + core) * 4 + x) * 2 + zlo) * 4 + yl) * 2 + y0


def all_places():
    return itertools.product(range(4), range(2), range(4), range(2), range(4), range(2))


def to_groups():
    return [
        (device_number(zhi, core, x, zlo, yl, y0), device_number(x, y0, zhi, zlo, yl, core))
        for zhi, core, x, zlo, yl, y0 in all_places()
    ]


def rows_to_groups(halo):
    pairs = []
    for zhi, core, x, zlo, yl, y0 in all_places():
        group = 2 * x + zlo + halo
        if zhi == 0 and core == y0 and group < 8:
            target = device_number(0, core, group // 2, zlo, yl, group % 2)
            pairs.append((device_number(0, core, x, zlo, yl, y0), target))
    return pairs


SWAP = [(1, 2), (2, 1)]


def site_start(sectors, slice_at, half):
    return jnp.clip(OWN * slice_at - BEFORE + HALF * half, 0, sectors - HALF)


def ops_pieces(ops_blocks, shift, core):
    sectors = ops_blocks.shape[0]
    target = jnp.arange(sectors, dtype=jnp.int32) + shift
    inside = (target >= 0) & (target < sectors)
    masked = jnp.where(inside[:, None, None], ops_blocks, jnp.zeros((), BF16))
    lower = jnp.concatenate([jnp.zeros_like(masked[:OWN]), masked[:-OWN]], 0)
    return jnp.where(core == 0, lower, masked).reshape(4, 2 * OWN, BLOCK, BLOCK)


def phase_kernel(sites, steps, n_in, sources, targets, with_ops, *refs):
    whole, part, mine, other = refs[:4]
    ins = refs[4 : 4 + n_in]
    outs = refs[4 + n_in : -2]
    site_at, sems = refs[-2:]
    core = whole[0]
    shift = whole[1]

    def copies(slot, site, source):
        return [
            pltpu.make_async_copy(
                source.at[(site // 2) * 2 + half],
                site_at.at[slot, :, pl.ds(whole[2 + half], HALF)],
                sems.at[slot, half],
            )
            for half in range(2)
        ]

    @pl.when(whole[2] != 0)
    def _():
        site_at[:, :, :BEFORE] = jnp.zeros((len(sites), STATES, BEFORE, BLOCK, BLOCK), BF16)

    @pl.when(whole[3] != HALF)
    def _():
        site_at[:, :, WINDOW - 1] = jnp.zeros((len(sites), STATES, BLOCK, BLOCK), BF16)

    for slot, site in enumerate(sites):
        @pl.when(core == site % 2)
        def _():
            for copy in copies(slot, site, mine):
                copy.start()

        @pl.when(core != site % 2)
        def _():
            for copy in copies(slot, site, other):
                copy.start()

    done_sites = set()
    state = {}

    def get(site, sector):
        if (site, sector) in state:
            return state[site, sector]
        where, index = sources[site, sector]
        return ins[where][index]

    for site, first in steps:
        slot = sites.index(site)
        if site not in done_sites:
            done_sites.add(site)
            for copy in copies(slot, site, mine):
                copy.wait()
        for sector in (first, first + 1):
            total = None
            for s in range(STATES):
                block = get(site, sector - s)
                ops, env = block[:, :BLOCK], block[:, BLOCK:]
                left = site_at[slot, s, sector + BEFORE]
                cross = site_at[slot, jnp.clip(s - shift, 0, 2), sector + BEFORE]
                half_env = jnp.dot(env, left, preferred_element_type=F32)
                if with_ops(site):
                    right = site_at[slot, s, sector + BEFORE + shift]
                    both = jnp.dot(ops, jnp.concatenate([right, cross], 1), preferred_element_type=F32)
                    image = jnp.concatenate(
                        [part[s] * both[:, :BLOCK], half_env + part[3 + s] * both[:, BLOCK:]], 1
                    )
                else:
                    image = half_env + part[3 + s] * jnp.dot(ops, cross, preferred_element_type=F32)
                product = lax.dot_general(
                    left, image.astype(BF16), (((0,), (0,)), ((), ())), preferred_element_type=F32
                )
                total = product if total is None else total + product
            total = total.astype(BF16)
            state[site + 1, sector] = total
            for which, index in targets[site + 1, sector]:
                outs[which][index] = total


def run_phase(sites, steps, ins, sources, outs, targets, with_ops, whole, part, mine, other):
    blocks = 2 * len(steps) * (15 if with_ops(sites[0]) else 9)
    return pl.pallas_call(
        functools.partial(phase_kernel, sites, steps, len(ins), sources, targets, with_ops),
        out_shape=[jax.ShapeDtypeStruct(shape, BF16) for shape in outs],
        in_specs=[pl.BlockSpec(memory_space=pltpu.SMEM)] * 2
        + [pl.BlockSpec(memory_space=pl.ANY)] * 2
        + [pl.BlockSpec(memory_space=pltpu.VMEM)] * len(ins),
        out_specs=[pl.BlockSpec(memory_space=pltpu.VMEM)] * len(outs),
        scratch_shapes=[
            pltpu.VMEM((len(sites), STATES, WINDOW, BLOCK, BLOCK), BF16),
            pltpu.SemaphoreType.DMA((len(sites), 2)),
        ],
        compiler_params=pltpu.CompilerParams(vmem_limit_bytes=32 * 1024 * 1024),
        cost_estimate=pl.CostEstimate(flops=blocks * 2 * BLOCK**3, bytes_accessed=4 << 20, transcendentals=0),
    )(whole, part, mine, other, *ins)


def take_piece(start, site, piece, taken, sems):
    rows = HALF * BLOCK
    first = pl.multiple_of(start[0] * BLOCK, BLOCK)
    inward = [
        pltpu.make_async_copy(site.at[0, s, pl.ds(first, rows)], taken.at[s], sems.at[0, s]) for s in range(STATES)
    ]
    outward = [pltpu.make_async_copy(taken.at[s], piece.at[s], sems.at[1, s]) for s in range(STATES)]
    for copy in inward:
        copy.start()
    for before, after in zip(inward, outward):
        before.wait()
        after.start()
    for copy in outward:
        copy.wait()


def add_cores(over, summed):
    for site in range(4):
        both = (over[0, site].astype(F32) + over[1, site].astype(F32)).astype(BF16)
        for piece in range(8):
            summed[site, piece % 2, piece // 2] = both[piece]


def add_columns(over, summed):
    total = over[0].astype(F32)
    for source in range(1, 32):
        total += over[source].astype(F32)
    summed[...] = total.astype(BF16)


def add_up(kernel, array, out):
    return pl.pallas_call(
        kernel,
        out_shape=jax.ShapeDtypeStruct(out, BF16),
        in_specs=[pl.BlockSpec(memory_space=pltpu.VMEM)],
        out_specs=pl.BlockSpec(memory_space=pltpu.VMEM),
        compiler_params=pltpu.CompilerParams(vmem_limit_bytes=16 << 20),
        cost_estimate=pl.CostEstimate(flops=1 << 19, bytes_accessed=2 << 20, transcendentals=0),
    )(array)


def body(site_tensor, term_ops, env_rows, term_shift, keep_weight, env_weight):
    sectors = site_tensor.shape[2] // BLOCK
    core = lax.axis_index("core")
    at_zlo, at_yl, at_y0 = (lax.axis_index(name) for name in ("zlo", "yl", "y0"))
    group = lax.axis_index("x") * 2 + at_y0

    start = site_start(sectors, group, at_zlo).astype(jnp.int32).reshape(1)
    piece = pl.pallas_call(
        take_piece,
        out_shape=jax.ShapeDtypeStruct((STATES, HALF * BLOCK, BLOCK), BF16),
        in_specs=[pl.BlockSpec(memory_space=pltpu.SMEM), pl.BlockSpec(memory_space=pltpu.HBM)],
        out_specs=pl.BlockSpec(memory_space=pltpu.HBM),
        scratch_shapes=[pltpu.VMEM((STATES, HALF * BLOCK, BLOCK), BF16), pltpu.SemaphoreType.DMA((2, STATES))],
        compiler_params=pltpu.CompilerParams(vmem_limit_bytes=60 << 20),
        cost_estimate=pl.CostEstimate(flops=0, bytes_accessed=800_000, transcendentals=0),
    )(start, site_tensor).reshape(STATES, HALF, BLOCK, BLOCK)
    mine = lax.all_gather(piece, ("zhi", "zlo"))
    spots = [site_start(sectors, group, half) - (OWN * group - BEFORE) for half in range(2)]

    pieces = ops_pieces(term_ops[0].reshape(sectors, BLOCK, BLOCK), term_shift[0], core)
    over = lax.all_to_all(pieces, "x", 0, 0)
    ops_now = lax.dynamic_index_in_dim(over, lax.axis_index("zhi"), 0, keepdims=False)
    ops_now = lax.ppermute(ops_now, ("core", "y0"), [(0, 0), (1, 2), (2, 1), (3, 3)])
    figures = jnp.concatenate([keep_weight[0], env_weight[0], term_shift.astype(F32), jnp.zeros((1,), F32)])
    figures = lax.ppermute(figures, AXES, to_groups())
    shift = figures[6].astype(jnp.int32)
    partner = jnp.arange(STATES, dtype=jnp.int32) - shift
    factors = jnp.where((partner >= 0) & (partner <= 2), figures[3:6], 0.0)
    part = jnp.concatenate([figures[:3], factors])
    whole = jnp.stack([core, shift] + spots).astype(jnp.int32)

    piece = lax.ppermute(env_rows, AXES, rows_to_groups(0))
    halo = lax.ppermute(env_rows, AXES, rows_to_groups(1))
    env_now = jnp.zeros((2 * OWN * BLOCK, BLOCK), BF16)
    spot = at_yl * BLOCK + core * (BLOCK // 2)
    env_now = lax.dynamic_update_slice_in_dim(env_now, halo, spot, 0)
    env_now = lax.dynamic_update_slice_in_dim(env_now, piece, spot + OWN * BLOCK, 0)
    window = jnp.concatenate([ops_now, env_now.reshape(2 * OWN, BLOCK, BLOCK)], 2)

    mine, window, whole, part = lax.optimization_barrier((mine, window, whole, part))
    other = lax.ppermute(mine, "core", [(0, 1), (1, 0)])

    wide = (BLOCK, 2 * BLOCK)
    onward = [(i, i + 1) for i in range(7)]

    def before_last(site):
        return site < 7

    sources = {(0, sector): (0, sector + OWN) for sector in range(-OWN, OWN)}
    targets = {(1, -2): [], (1, -1): []}
    for sector in range(OWN):
        targets[1, sector] = [(0, sector)]
        targets[2, sector] = [(1, sector)] + ([(3, (0, sector - 2))] if sector >= 2 else [])
    for sector in (2, 3):
        targets[3, sector] = [(2, sector - 2), (3, (1, sector - 2))]
    first, full, upper, tails = run_phase(
        [0, 1, 2],
        [(0, 0), (0, 2), (0, -2), (1, 2), (1, 0), (2, 2)],
        [window],
        sources,
        [(OWN,) + wide, (OWN,) + wide, (2,) + wide, (2, 2) + wide],
        targets,
        before_last,
        whole,
        part,
        mine,
        other,
    )
    bonds = [first[:, :, BLOCK:], full[:, :, BLOCK:]]
    for site in (2, 4, 6):
        tails = lax.ppermute(tails, ("x", "y0"), onward)
        last = site == 6
        sources = {}
        for sector in (-2, -1):
            sources[site, sector] = (2, (0, sector + 2))
            sources[site + 1, sector] = (2, (1, sector + 2))
        for sector in range(OWN):
            sources[site, sector] = (0, sector)
        for sector in (2, 3):
            sources[site + 1, sector] = (1, sector - 2)
        targets = {}
        for sector in (0, 1):
            targets[site + 1, sector] = [(0, sector)]
        for sector in range(OWN):
            targets[site + 2, sector] = [(1, sector)]
        steps = [(site, 0), (site + 1, 2), (site + 1, 0)]
        outs = [(2,) + wide, (OWN,) + ((BLOCK, BLOCK) if last else wide)]
        if not last:
            for sector in (2, 3):
                targets[site + 2, sector].append((3, (0, sector - 2)))
                targets[site + 3, sector] = [(2, sector - 2), (3, (1, sector - 2))]
            steps.append((site + 2, 2))
            outs += [(2,) + wide, (2, 2) + wide]
        old_upper = upper
        lower, full, *rest = run_phase(
            [site, site + 1] + ([] if last else [site + 2]),
            steps,
            [full, upper, tails],
            sources,
            outs,
            targets,
            before_last,
            whole,
            part,
            mine,
            other,
        )
        bonds += [lower[:, :, BLOCK:], old_upper[:, :, BLOCK:], full if last else full[:, :, BLOCK:]]
        if not last:
            upper, tails = rest

    partial = jnp.concatenate(bonds, 0).reshape(4, 2, 8, BLOCK // 2, BLOCK).transpose(1, 0, 2, 3, 4)
    over = lax.all_to_all(partial, "core", 0, 0)
    summed = add_up(add_cores, over, (4, 2, 4, BLOCK // 2, BLOCK)).reshape(32, BLOCK // 2, BLOCK)
    over = lax.all_to_all(summed, ("zhi", "zlo", "yl"), 0, 0)
    summed = add_up(add_columns, over, (BLOCK // 2, BLOCK))
    swapped = lax.ppermute(summed, ("zlo", "y0"), SWAP)
    return jnp.where(at_zlo == at_y0, summed, swapped)[None]


def solution(mesh):
    parts = Mesh(mesh.devices.reshape(4, 2, 4, 2, 4, 2), AXES)
    seg, op = ("zhi", "core"), ("x", "zlo", "yl", "y0")
    placed = (P(seg, None, None, None), P(op, None, None), P(op, None), P(op), P(op, None), P(op, None))
    return jax.shard_map(body, mesh=parts, in_specs=placed, out_specs=P(seg, op, None), check_vma=False)
```

```python
import functools
import itertools

import jax
import jax.numpy as jnp
from jax import lax
from jax.experimental import pallas as pl
from jax.experimental.pallas import tpu as pltpu
from jax.sharding import Mesh, PartitionSpec as P

BLOCK = 128
OWN = 4
HALF = 4
WINDOW = 2 * HALF
BEFORE = 3
STATES = 3
AXES = ("zhi", "core", "x", "zlo", "yl", "y0")
BF16 = jnp.bfloat16
F32 = jnp.float32


def device_number(zhi, core, x, zlo, yl, y0):
    return ((((zhi * 2 + core) * 4 + x) * 2 + zlo) * 4 + yl) * 2 + y0


def all_places():
    return itertools.product(range(4), range(2), range(4), range(2), range(4), range(2))


def to_groups():
    return [
        (device_number(zhi, core, x, zlo, yl, y0), device_number(x, y0, zhi, zlo, yl, core))
        for zhi, core, x, zlo, yl, y0 in all_places()
    ]


def rows_to_groups(halo):
    pairs = []
    for zhi, core, x, zlo, yl, y0 in all_places():
        group = 2 * x + zlo + halo
        if zhi == 0 and core == y0 and group < 8:
            target = device_number(0, core, group // 2, zlo, yl, group % 2)
            pairs.append((device_number(0, core, x, zlo, yl, y0), target))
    return pairs


def site_start(sectors, slice_at, half):
    return jnp.clip(OWN * slice_at - BEFORE + HALF * half, 0, sectors - HALF)


def ops_pieces(ops_blocks, shift, core):
    sectors = ops_blocks.shape[0]
    target = jnp.arange(sectors, dtype=jnp.int32) + shift
    inside = (target >= 0) & (target < sectors)
    masked = jnp.where(inside[:, None, None], ops_blocks, jnp.zeros((), BF16))
    lower = jnp.concatenate([jnp.zeros_like(masked[:OWN]), masked[:-OWN]], 0)
    return jnp.where(core == 0, lower, masked).reshape(4, 2 * OWN, BLOCK, BLOCK)


def phase_kernel(sites, steps, halves, n_in, sources, targets, with_ops, *refs):
    whole, part = refs[:2]
    blocks = dict(zip(halves, zip(refs[2::2], refs[3::2])))
    refs = refs[2 + 2 * len(halves) :]
    ins = refs[:n_in]
    outs = refs[n_in:-2]
    site_at, sems = refs[-2:]
    core = whole[0]
    shift = whole[1]

    def copies(slot, site, which):
        source = blocks[site // 4][which]
        return [
            pltpu.make_async_copy(
                source.at[(site % 4 // 2) * 2 + half],
                site_at.at[slot, :, pl.ds(whole[2 + half], HALF)],
                sems.at[slot, half],
            )
            for half in range(2)
        ]

    @pl.when(whole[2] != 0)
    def _():
        site_at[:, :, :BEFORE] = jnp.zeros((len(sites), STATES, BEFORE, BLOCK, BLOCK), BF16)

    @pl.when(whole[3] != HALF)
    def _():
        site_at[:, :, WINDOW - 1] = jnp.zeros((len(sites), STATES, BLOCK, BLOCK), BF16)

    for slot, site in enumerate(sites):
        @pl.when(core == site % 2)
        def _():
            for copy in copies(slot, site, 0):
                copy.start()

        @pl.when(core != site % 2)
        def _():
            for copy in copies(slot, site, 1):
                copy.start()

    done_sites = set()
    state = {}

    def get(site, sector):
        if (site, sector) in state:
            return state[site, sector]
        where, index = sources[site, sector]
        return ins[where][index]

    for site, first in steps:
        slot = sites.index(site)
        if site not in done_sites:
            done_sites.add(site)
            for copy in copies(slot, site, 0):
                copy.wait()
        for sector in (first, first + 1):
            total = None
            for s in range(STATES):
                left = site_at[slot, s, sector + BEFORE]
                cross = site_at[slot, jnp.clip(s - shift, 0, 2), sector + BEFORE]
                cross = (part[3 + s] * cross.astype(F32)).astype(BF16)
                if with_ops(site):
                    right = site_at[slot, s, sector + BEFORE + shift]
                    upper = jnp.concatenate([right, cross], 1)
                    lower = jnp.concatenate([jnp.zeros_like(left), left], 1)
                else:
                    upper, lower = cross, left
                image = jnp.dot(
                    get(site, sector - s), jnp.concatenate([upper, lower], 0), preferred_element_type=F32
                )
                if with_ops(site):
                    image = jnp.concatenate([part[s] * image[:, :BLOCK], image[:, BLOCK:]], 1)
                product = lax.dot_general(
                    left, image.astype(BF16), (((0,), (0,)), ((), ())), preferred_element_type=F32
                )
                total = product if total is None else total + product
            total = total.astype(BF16)
            state[site + 1, sector] = total
            for which, index in targets[site + 1, sector]:
                outs[which][index] = total


def run_phase(sites, steps, ins, sources, outs, targets, with_ops, whole, part, pairs):
    halves = sorted({site // 4 for site in sites})
    blocks = 2 * len(steps) * (15 if with_ops(sites[0]) else 9)
    return pl.pallas_call(
        functools.partial(phase_kernel, sites, steps, halves, len(ins), sources, targets, with_ops),
        out_shape=[jax.ShapeDtypeStruct(shape, BF16) for shape in outs],
        in_specs=[pl.BlockSpec(memory_space=pltpu.SMEM)] * 2
        + [pl.BlockSpec(memory_space=pl.ANY)] * (2 * len(halves))
        + [pl.BlockSpec(memory_space=pltpu.VMEM)] * len(ins),
        out_specs=[pl.BlockSpec(memory_space=pltpu.VMEM)] * len(outs),
        scratch_shapes=[
            pltpu.VMEM((len(sites), STATES, WINDOW, BLOCK, BLOCK), BF16),
            pltpu.SemaphoreType.DMA((len(sites), 2)),
        ],
        compiler_params=pltpu.CompilerParams(vmem_limit_bytes=32 * 1024 * 1024),
        cost_estimate=pl.CostEstimate(flops=blocks * 2 * BLOCK**3, bytes_accessed=4 << 20, transcendentals=0),
    )(whole, part, *(array for half in halves for array in pairs[half]), *ins)


def take_piece(start, site, piece, taken, sems):
    rows = HALF * BLOCK
    first = pl.multiple_of(start[0] * BLOCK, BLOCK)
    inward = [
        pltpu.make_async_copy(site.at[0, s, pl.ds(first, rows)], taken.at[s], sems.at[0, s]) for s in range(STATES)
    ]
    outward = [pltpu.make_async_copy(taken.at[s], piece.at[s], sems.at[1, s]) for s in range(STATES)]
    for copy in inward:
        copy.start()
    for before, after in zip(inward, outward):
        before.wait()
        after.start()
    for copy in outward:
        copy.wait()


def add_cores(place, over, summed):
    for site in range(4):
        both = (over[0, site].astype(F32) + over[1, site].astype(F32)).astype(BF16)
        for zlo in range(2):
            summed[site, zlo] = jnp.where(place[0] == zlo, both, jnp.zeros_like(both))


def add_columns(over, summed):
    total = over[0].astype(F32)
    for source in range(1, 64):
        total += over[source].astype(F32)
    summed[...] = total.astype(BF16)


def add_up(kernel, ins, out):
    spaces = [pltpu.SMEM if array.ndim == 1 else pltpu.VMEM for array in ins]
    return pl.pallas_call(
        kernel,
        out_shape=jax.ShapeDtypeStruct(out, BF16),
        in_specs=[pl.BlockSpec(memory_space=space) for space in spaces],
        out_specs=pl.BlockSpec(memory_space=pltpu.VMEM),
        compiler_params=pltpu.CompilerParams(vmem_limit_bytes=16 << 20),
        cost_estimate=pl.CostEstimate(flops=1 << 19, bytes_accessed=2 << 20, transcendentals=0),
    )(*ins)


def body(site_tensor, term_ops, env_rows, term_shift, keep_weight, env_weight):
    sectors = site_tensor.shape[2] // BLOCK
    core = lax.axis_index("core")
    at_zlo, at_yl, at_y0 = (lax.axis_index(name) for name in ("zlo", "yl", "y0"))
    group = lax.axis_index("x") * 2 + at_y0

    start = site_start(sectors, group, at_zlo).astype(jnp.int32).reshape(1)
    piece = pl.pallas_call(
        take_piece,
        out_shape=jax.ShapeDtypeStruct((STATES, HALF * BLOCK, BLOCK), BF16),
        in_specs=[pl.BlockSpec(memory_space=pltpu.SMEM), pl.BlockSpec(memory_space=pltpu.HBM)],
        out_specs=pl.BlockSpec(memory_space=pltpu.HBM),
        scratch_shapes=[pltpu.VMEM((STATES, HALF * BLOCK, BLOCK), BF16), pltpu.SemaphoreType.DMA((2, STATES))],
        compiler_params=pltpu.CompilerParams(vmem_limit_bytes=60 << 20),
        cost_estimate=pl.CostEstimate(flops=0, bytes_accessed=800_000, transcendentals=0),
    )(start, site_tensor).reshape(STATES, HALF, BLOCK, BLOCK)
    mine = lax.all_gather(piece, ("zhi", "zlo"))
    spots = [site_start(sectors, group, half) - (OWN * group - BEFORE) for half in range(2)]

    pieces = ops_pieces(term_ops[0].reshape(sectors, BLOCK, BLOCK), term_shift[0], core)
    over = lax.all_to_all(pieces, "x", 0, 0)
    ops_now = lax.dynamic_index_in_dim(over, lax.axis_index("zhi"), 0, keepdims=False)
    ops_now = lax.ppermute(ops_now, ("core", "y0"), [(0, 0), (1, 2), (2, 1), (3, 3)])
    figures = jnp.concatenate([keep_weight[0], env_weight[0], term_shift.astype(F32), jnp.zeros((1,), F32)])
    figures = lax.ppermute(figures, AXES, to_groups())
    shift = figures[6].astype(jnp.int32)
    partner = jnp.arange(STATES, dtype=jnp.int32) - shift
    factors = jnp.where((partner >= 0) & (partner <= 2), figures[3:6], 0.0)
    part = jnp.concatenate([figures[:3], factors])
    whole = jnp.stack([core, shift] + spots).astype(jnp.int32)

    piece = lax.ppermute(env_rows, AXES, rows_to_groups(0))
    halo = lax.ppermute(env_rows, AXES, rows_to_groups(1))
    env_now = jnp.zeros((2 * OWN * BLOCK, BLOCK), BF16)
    spot = at_yl * BLOCK + core * (BLOCK // 2)
    env_now = lax.dynamic_update_slice_in_dim(env_now, halo, spot, 0)
    env_now = lax.dynamic_update_slice_in_dim(env_now, piece, spot + OWN * BLOCK, 0)
    window = jnp.concatenate([ops_now, env_now.reshape(2 * OWN, BLOCK, BLOCK)], 2)

    mine, window, whole, part = lax.optimization_barrier((mine, window, whole, part))
    mine_low, mine_high = mine[:4], mine[4:]
    pairs = [(mine_low, lax.ppermute(mine_low, "core", [(0, 1), (1, 0)]))]

    wide = (BLOCK, 2 * BLOCK)
    onward = [(i, i + 1) for i in range(7)]

    def before_last(site):
        return site < 7

    sources = {(0, sector): (0, sector + OWN) for sector in range(-OWN, OWN)}
    targets = {(1, -2): [], (1, -1): []}
    for sector in range(OWN):
        targets[1, sector] = [(0, sector)]
        targets[2, sector] = [(1, sector)] + ([(3, (0, sector - 2))] if sector >= 2 else [])
    for sector in (2, 3):
        targets[3, sector] = [(2, sector - 2), (3, (1, sector - 2))]
    first, full, upper, tails = run_phase(
        [0, 1, 2],
        [(0, 0), (0, 2), (0, -2), (1, 2), (1, 0), (2, 2)],
        [window],
        sources,
        [(OWN,) + wide, (OWN,) + wide, (2,) + wide, (2, 2) + wide],
        targets,
        before_last,
        whole,
        part,
        pairs,
    )
    mine_high, tails = lax.optimization_barrier((mine_high, tails))
    pairs.append((mine_high, lax.ppermute(mine_high, "core", [(0, 1), (1, 0)])))
    bonds = [first[:, :, BLOCK:], full[:, :, BLOCK:]]
    for site in (2, 4, 6):
        tails = lax.ppermute(tails, ("x", "y0"), onward)
        last = site == 6
        sources = {}
        for sector in (-2, -1):
            sources[site, sector] = (2, (0, sector + 2))
            sources[site + 1, sector] = (2, (1, sector + 2))
        for sector in range(OWN):
            sources[site, sector] = (0, sector)
        for sector in (2, 3):
            sources[site + 1, sector] = (1, sector - 2)
        targets = {}
        for sector in (0, 1):
            targets[site + 1, sector] = [(0, sector)]
        for sector in range(OWN):
            targets[site + 2, sector] = [(1, sector)]
        steps = [(site, 0), (site + 1, 2), (site + 1, 0)]
        outs = [(2,) + wide, (OWN,) + ((BLOCK, BLOCK) if last else wide)]
        if not last:
            for sector in (2, 3):
                targets[site + 2, sector].append((3, (0, sector - 2)))
                targets[site + 3, sector] = [(2, sector - 2), (3, (1, sector - 2))]
            steps.append((site + 2, 2))
            outs += [(2,) + wide, (2, 2) + wide]
        old_upper = upper
        lower, full, *rest = run_phase(
            [site, site + 1] + ([] if last else [site + 2]),
            steps,
            [full, upper, tails],
            sources,
            outs,
            targets,
            before_last,
            whole,
            part,
            pairs,
        )
        bonds += [lower[:, :, BLOCK:], old_upper[:, :, BLOCK:], full if last else full[:, :, BLOCK:]]
        if not last:
            upper, tails = rest

    partial = jnp.concatenate(bonds, 0).reshape(4, 2, 8, BLOCK // 2, BLOCK).transpose(1, 0, 2, 3, 4)
    over = lax.all_to_all(partial, "core", 0, 0)
    place = at_y0.astype(jnp.int32).reshape(1)
    summed = add_up(add_cores, [place, over], (4, 2, 8, BLOCK // 2, BLOCK)).reshape(64, BLOCK // 2, BLOCK)
    over = lax.all_to_all(summed, ("zhi", "zlo", "yl", "y0"), 0, 0)
    return add_up(add_columns, [over], (BLOCK // 2, BLOCK))[None]


def solution(mesh):
    parts = Mesh(mesh.devices.reshape(4, 2, 4, 2, 4, 2), AXES)
    seg, op = ("zhi", "core"), ("x", "zlo", "yl", "y0")
    placed = (P(seg, None, None, None), P(op, None, None), P(op, None), P(op), P(op, None), P(op, None))
    return jax.shard_map(body, mesh=parts, in_specs=placed, out_specs=P(seg, op, None), check_vma=False)
```

```python
import functools
import itertools

import jax
import jax.numpy as jnp
from jax import lax
from jax.experimental import pallas as pl
from jax.experimental.pallas import tpu as pltpu
from jax.sharding import Mesh, PartitionSpec as P

BLOCK = 128
OWN = 4
HALF = 4
WINDOW = 2 * HALF
BEFORE = 3
STATES = 3
AXES = ("zhi", "core", "x", "zlo", "yl", "y0")
BF16 = jnp.bfloat16
F32 = jnp.float32


def device_number(zhi, core, x, zlo, yl, y0):
    return ((((zhi * 2 + core) * 4 + x) * 2 + zlo) * 4 + yl) * 2 + y0


def all_places():
    return itertools.product(range(4), range(2), range(4), range(2), range(4), range(2))


def to_groups():
    return [
        (device_number(zhi, core, x, zlo, yl, y0), device_number(x, y0, zhi, zlo, yl, core))
        for zhi, core, x, zlo, yl, y0 in all_places()
    ]


def rows_to_groups(halo):
    pairs = []
    for zhi, core, x, zlo, yl, y0 in all_places():
        group = 2 * x + zlo + halo
        if zhi == 0 and core == y0 and group < 8:
            target = device_number(0, core, group // 2, zlo, yl, group % 2)
            pairs.append((device_number(0, core, x, zlo, yl, y0), target))
    return pairs


SWAP = [(1, 2), (2, 1)]


def site_start(sectors, slice_at, half):
    return jnp.clip(OWN * slice_at - BEFORE + HALF * half, 0, sectors - HALF)


def ops_pieces(ops_blocks, shift, core):
    sectors = ops_blocks.shape[0]
    target = jnp.arange(sectors, dtype=jnp.int32) + shift
    inside = (target >= 0) & (target < sectors)
    masked = jnp.where(inside[:, None, None], ops_blocks, jnp.zeros((), BF16))
    lower = jnp.concatenate([jnp.zeros_like(masked[:OWN]), masked[:-OWN]], 0)
    return jnp.where(core == 0, lower, masked).reshape(4, 2 * OWN, BLOCK, BLOCK)


def phase_kernel(sites, steps, n_in, sources, targets, with_ops, *refs):
    whole, part, mine, other = refs[:4]
    ins = refs[4 : 4 + n_in]
    outs = refs[4 + n_in : -2]
    site_at, sems = refs[-2:]
    core = whole[0]
    shift = whole[1]

    def copies(slot, site, source):
        return [
            pltpu.make_async_copy(
                source.at[(site // 2) * 2 + half],
                site_at.at[slot, :, pl.ds(whole[2 + half], HALF)],
                sems.at[slot, half],
            )
            for half in range(2)
        ]

    @pl.when(whole[2] != 0)
    def _():
        site_at[:, :, :BEFORE] = jnp.zeros((len(sites), STATES, BEFORE, BLOCK, BLOCK), BF16)

    @pl.when(whole[3] != HALF)
    def _():
        site_at[:, :, WINDOW - 1] = jnp.zeros((len(sites), STATES, BLOCK, BLOCK), BF16)

    for slot, site in enumerate(sites):
        @pl.when(core == site % 2)
        def _():
            for copy in copies(slot, site, mine):
                copy.start()

        @pl.when(core != site % 2)
        def _():
            for copy in copies(slot, site, other):
                copy.start()

    done_sites = set()
    state = {}

    def get(site, sector):
        if (site, sector) in state:
            return state[site, sector]
        where, index = sources[site, sector]
        return ins[where][index]

    for site, first in steps:
        slot = sites.index(site)
        if site not in done_sites:
            done_sites.add(site)
            for copy in copies(slot, site, mine):
                copy.wait()
        for sector in (first, first + 1):
            total = None
            for s in range(STATES):
                left = site_at[slot, s, sector + BEFORE]
                cross = site_at[slot, jnp.clip(s - shift, 0, 2), sector + BEFORE]
                cross = (part[3 + s] * cross.astype(F32)).astype(BF16)
                if with_ops(site):
                    right = site_at[slot, s, sector + BEFORE + shift]
                    upper = jnp.concatenate([right, cross], 1)
                    lower = jnp.concatenate([jnp.zeros_like(left), left], 1)
                else:
                    upper, lower = cross, left
                image = jnp.dot(
                    get(site, sector - s), jnp.concatenate([upper, lower], 0), preferred_element_type=F32
                )
                if with_ops(site):
                    image = jnp.concatenate([part[s] * image[:, :BLOCK], image[:, BLOCK:]], 1)
                product = lax.dot_general(
                    left, image.astype(BF16), (((0,), (0,)), ((), ())), preferred_element_type=F32
                )
                total = product if total is None else total + product
            total = total.astype(BF16)
            state[site + 1, sector] = total
            for which, index in targets[site + 1, sector]:
                outs[which][index] = total


def run_phase(sites, steps, ins, sources, outs, targets, with_ops, whole, part, mine, other):
    blocks = 2 * len(steps) * (15 if with_ops(sites[0]) else 9)
    return pl.pallas_call(
        functools.partial(phase_kernel, sites, steps, len(ins), sources, targets, with_ops),
        out_shape=[jax.ShapeDtypeStruct(shape, BF16) for shape in outs],
        in_specs=[pl.BlockSpec(memory_space=pltpu.SMEM)] * 2
        + [pl.BlockSpec(memory_space=pl.ANY)] * 2
        + [pl.BlockSpec(memory_space=pltpu.VMEM)] * len(ins),
        out_specs=[pl.BlockSpec(memory_space=pltpu.VMEM)] * len(outs),
        scratch_shapes=[
            pltpu.VMEM((len(sites), STATES, WINDOW, BLOCK, BLOCK), BF16),
            pltpu.SemaphoreType.DMA((len(sites), 2)),
        ],
        compiler_params=pltpu.CompilerParams(vmem_limit_bytes=32 * 1024 * 1024),
        cost_estimate=pl.CostEstimate(flops=blocks * 2 * BLOCK**3, bytes_accessed=4 << 20, transcendentals=0),
    )(whole, part, mine, other, *ins)


def take_piece(start, site, piece, taken, sems):
    rows = HALF * BLOCK
    first = pl.multiple_of(start[0] * BLOCK, BLOCK)
    inward = [
        pltpu.make_async_copy(site.at[0, s, pl.ds(first, rows)], taken.at[s], sems.at[0, s]) for s in range(STATES)
    ]
    outward = [pltpu.make_async_copy(taken.at[s], piece.at[s], sems.at[1, s]) for s in range(STATES)]
    for copy in inward:
        copy.start()
    for before, after in zip(inward, outward):
        before.wait()
        after.start()
    for copy in outward:
        copy.wait()


def bring(blocks, held, sem):
    copy = pltpu.make_async_copy(blocks, held, sem)
    copy.start()
    copy.wait()


def add_cores(over, summed):
    for site in range(4):
        both = (over[0, site].astype(F32) + over[1, site].astype(F32)).astype(BF16)
        for piece in range(8):
            summed[site, piece % 2, piece // 2] = both[piece]


def add_columns(over, summed):
    total = over[0].astype(F32)
    for source in range(1, 32):
        total += over[source].astype(F32)
    summed[...] = total.astype(BF16)


def add_up(kernel, array, out):
    return pl.pallas_call(
        kernel,
        out_shape=jax.ShapeDtypeStruct(out, BF16),
        in_specs=[pl.BlockSpec(memory_space=pltpu.VMEM)],
        out_specs=pl.BlockSpec(memory_space=pltpu.VMEM),
        compiler_params=pltpu.CompilerParams(vmem_limit_bytes=16 << 20),
        cost_estimate=pl.CostEstimate(flops=1 << 19, bytes_accessed=2 << 20, transcendentals=0),
    )(array)


def body(site_tensor, term_ops, env_rows, term_shift, keep_weight, env_weight):
    sectors = site_tensor.shape[2] // BLOCK
    core = lax.axis_index("core")
    at_zlo, at_yl, at_y0 = (lax.axis_index(name) for name in ("zlo", "yl", "y0"))
    group = lax.axis_index("x") * 2 + at_y0

    start = site_start(sectors, group, at_zlo).astype(jnp.int32).reshape(1)
    piece = pl.pallas_call(
        take_piece,
        out_shape=jax.ShapeDtypeStruct((STATES, HALF * BLOCK, BLOCK), BF16),
        in_specs=[pl.BlockSpec(memory_space=pltpu.SMEM), pl.BlockSpec(memory_space=pltpu.HBM)],
        out_specs=pl.BlockSpec(memory_space=pltpu.HBM),
        scratch_shapes=[pltpu.VMEM((STATES, HALF * BLOCK, BLOCK), BF16), pltpu.SemaphoreType.DMA((2, STATES))],
        compiler_params=pltpu.CompilerParams(vmem_limit_bytes=60 << 20),
        cost_estimate=pl.CostEstimate(flops=0, bytes_accessed=800_000, transcendentals=0),
    )(start, site_tensor).reshape(STATES, HALF, BLOCK, BLOCK)
    mine = lax.all_gather(piece, ("zhi", "zlo"))
    spots = [site_start(sectors, group, half) - (OWN * group - BEFORE) for half in range(2)]

    pieces = ops_pieces(term_ops[0].reshape(sectors, BLOCK, BLOCK), term_shift[0], core)
    over = lax.all_to_all(pieces, "x", 0, 0)
    ops_now = lax.dynamic_index_in_dim(over, lax.axis_index("zhi"), 0, keepdims=False)
    ops_now = lax.ppermute(ops_now, ("core", "y0"), [(0, 0), (1, 2), (2, 1), (3, 3)])
    figures = jnp.concatenate([keep_weight[0], env_weight[0], term_shift.astype(F32), jnp.zeros((1,), F32)])
    figures = lax.ppermute(figures, AXES, to_groups())
    shift = figures[6].astype(jnp.int32)
    partner = jnp.arange(STATES, dtype=jnp.int32) - shift
    factors = jnp.where((partner >= 0) & (partner <= 2), figures[3:6], 0.0)
    part = jnp.concatenate([figures[:3], factors])
    whole = jnp.stack([core, shift] + spots).astype(jnp.int32)

    piece = lax.ppermute(env_rows, AXES, rows_to_groups(0))
    halo = lax.ppermute(env_rows, AXES, rows_to_groups(1))
    env_now = jnp.zeros((2 * OWN * BLOCK, BLOCK), BF16)
    spot = at_yl * BLOCK + core * (BLOCK // 2)
    env_now = lax.dynamic_update_slice_in_dim(env_now, halo, spot, 0)
    env_now = lax.dynamic_update_slice_in_dim(env_now, piece, spot + OWN * BLOCK, 0)
    window = jnp.concatenate([ops_now, env_now.reshape(2 * OWN, BLOCK, BLOCK)], 2)

    mine, window, whole, part = lax.optimization_barrier((mine, window, whole, part))
    other = lax.ppermute(mine, "core", [(0, 1), (1, 0)])
    mine = pl.pallas_call(
        bring,
        out_shape=jax.ShapeDtypeStruct(mine.shape, BF16),
        in_specs=[pl.BlockSpec(memory_space=pl.ANY)],
        out_specs=pl.BlockSpec(memory_space=pltpu.VMEM),
        scratch_shapes=[pltpu.SemaphoreType.DMA],
        compiler_params=pltpu.CompilerParams(vmem_limit_bytes=16 << 20),
        cost_estimate=pl.CostEstimate(flops=0, bytes_accessed=6 << 20, transcendentals=0),
    )(mine)

    wide = (BLOCK, 2 * BLOCK)
    onward = [(i, i + 1) for i in range(7)]

    def before_last(site):
        return site < 7

    sources = {(0, sector): (0, sector + OWN) for sector in range(-OWN, OWN)}
    targets = {(1, -2): [], (1, -1): []}
    for sector in range(OWN):
        targets[1, sector] = [(0, sector)]
        targets[2, sector] = [(1, sector)] + ([(3, (0, sector - 2))] if sector >= 2 else [])
    for sector in (2, 3):
        targets[3, sector] = [(2, sector - 2), (3, (1, sector - 2))]
    first, full, upper, tails = run_phase(
        [0, 1, 2],
        [(0, 0), (0, 2), (0, -2), (1, 2), (1, 0), (2, 2)],
        [window],
        sources,
        [(OWN,) + wide, (OWN,) + wide, (2,) + wide, (2, 2) + wide],
        targets,
        before_last,
        whole,
        part,
        mine,
        other,
    )
    bonds = [first[:, :, BLOCK:], full[:, :, BLOCK:]]
    for site in (2, 4, 6):
        tails = lax.ppermute(tails, ("x", "y0"), onward)
        last = site == 6
        sources = {}
        for sector in (-2, -1):
            sources[site, sector] = (2, (0, sector + 2))
            sources[site + 1, sector] = (2, (1, sector + 2))
        for sector in range(OWN):
            sources[site, sector] = (0, sector)
        for sector in (2, 3):
            sources[site + 1, sector] = (1, sector - 2)
        targets = {}
        for sector in (0, 1):
            targets[site + 1, sector] = [(0, sector)]
        for sector in range(OWN):
            targets[site + 2, sector] = [(1, sector)]
        steps = [(site, 0), (site + 1, 2), (site + 1, 0)]
        outs = [(2,) + wide, (OWN,) + ((BLOCK, BLOCK) if last else wide)]
        if not last:
            for sector in (2, 3):
                targets[site + 2, sector].append((3, (0, sector - 2)))
                targets[site + 3, sector] = [(2, sector - 2), (3, (1, sector - 2))]
            steps.append((site + 2, 2))
            outs += [(2,) + wide, (2, 2) + wide]
        old_upper = upper
        lower, full, *rest = run_phase(
            [site, site + 1] + ([] if last else [site + 2]),
            steps,
            [full, upper, tails],
            sources,
            outs,
            targets,
            before_last,
            whole,
            part,
            mine,
            other,
        )
        bonds += [lower[:, :, BLOCK:], old_upper[:, :, BLOCK:], full if last else full[:, :, BLOCK:]]
        if not last:
            upper, tails = rest

    partial = jnp.concatenate(bonds, 0).reshape(4, 2, 8, BLOCK // 2, BLOCK).transpose(1, 0, 2, 3, 4)
    over = lax.all_to_all(partial, "core", 0, 0)
    summed = add_up(add_cores, over, (4, 2, 4, BLOCK // 2, BLOCK)).reshape(32, BLOCK // 2, BLOCK)
    over = lax.all_to_all(summed, ("zhi", "zlo", "yl"), 0, 0)
    summed = add_up(add_columns, over, (BLOCK // 2, BLOCK))
    swapped = lax.ppermute(summed, ("zlo", "y0"), SWAP)
    return jnp.where(at_zlo == at_y0, summed, swapped)[None]


def solution(mesh):
    parts = Mesh(mesh.devices.reshape(4, 2, 4, 2, 4, 2), AXES)
    seg, op = ("zhi", "core"), ("x", "zlo", "yl", "y0")
    placed = (P(seg, None, None, None), P(op, None, None), P(op, None), P(op), P(op, None), P(op, None))
    return jax.shard_map(body, mesh=parts, in_specs=placed, out_specs=P(seg, op, None), check_vma=False)
```

```python
import functools
import itertools

import jax
import jax.numpy as jnp
from jax import lax
from jax.experimental import pallas as pl
from jax.experimental.pallas import tpu as pltpu
from jax.sharding import Mesh, PartitionSpec as P

BLOCK = 128
OWN = 4
HALF = 4
WINDOW = 2 * HALF
BEFORE = 3
STATES = 3
AXES = ("zhi", "core", "x", "zlo", "yl", "y0")
BF16 = jnp.bfloat16
F32 = jnp.float32


def device_number(zhi, core, x, zlo, yl, y0):
    return ((((zhi * 2 + core) * 4 + x) * 2 + zlo) * 4 + yl) * 2 + y0


def all_places():
    return itertools.product(range(4), range(2), range(4), range(2), range(4), range(2))


def to_groups():
    return [
        (device_number(zhi, core, x, zlo, yl, y0), device_number(x, y0, zhi, zlo, yl, core))
        for zhi, core, x, zlo, yl, y0 in all_places()
    ]


def rows_to_groups(halo):
    pairs = []
    for zhi, core, x, zlo, yl, y0 in all_places():
        group = 2 * x + zlo + halo
        if zhi == 0 and core == y0 and group < 8:
            target = device_number(0, core, group // 2, zlo, yl, group % 2)
            pairs.append((device_number(0, core, x, zlo, yl, y0), target))
    return pairs


SWAP = [(1, 2), (2, 1)]


def site_start(sectors, slice_at, half):
    return jnp.clip(OWN * slice_at - BEFORE + HALF * half, 0, sectors - HALF)


def ops_pieces(ops_blocks, shift, core):
    sectors = ops_blocks.shape[0]
    target = jnp.arange(sectors, dtype=jnp.int32) + shift
    inside = (target >= 0) & (target < sectors)
    masked = jnp.where(inside[:, None, None], ops_blocks, jnp.zeros((), BF16))
    lower = jnp.concatenate([jnp.zeros_like(masked[:OWN]), masked[:-OWN]], 0)
    return jnp.where(core == 0, lower, masked).reshape(4, 2 * OWN, BLOCK, BLOCK)


def phase_kernel(sites, steps, n_in, sources, targets, with_ops, *refs):
    whole, part, mine, other = refs[:4]
    ins = refs[4 : 4 + n_in]
    outs = refs[4 + n_in : -2]
    site_at, sems = refs[-2:]
    core = whole[0]
    shift = whole[1]

    def copies(slot, site, source):
        return [
            pltpu.make_async_copy(
                source.at[(site // 2) * 2 + half],
                site_at.at[slot, :, pl.ds(whole[2 + half], HALF)],
                sems.at[slot, half],
            )
            for half in range(2)
        ]

    @pl.when(whole[2] != 0)
    def _():
        site_at[:, :, :BEFORE] = jnp.zeros((len(sites), STATES, BEFORE, BLOCK, BLOCK), BF16)

    @pl.when(whole[3] != HALF)
    def _():
        site_at[:, :, WINDOW - 1] = jnp.zeros((len(sites), STATES, BLOCK, BLOCK), BF16)

    for slot, site in enumerate(sites):
        @pl.when(core == site % 2)
        def _():
            for copy in copies(slot, site, mine):
                copy.start()

        @pl.when(core != site % 2)
        def _():
            for copy in copies(slot, site, other):
                copy.start()

    state = {}

    def get(site, sector):
        if (site, sector) in state:
            return state[site, sector]
        where, index = sources[site, sector]
        return ins[where][index]

    for site, sectors in steps:
        slot = sites.index(site)
        for copy in copies(slot, site, mine):
            copy.wait()
        lefts, images = {}, {}
        for sector in sectors:
            for s in range(STATES):
                left = site_at[slot, s, sector + BEFORE]
                cross = site_at[slot, jnp.clip(s - shift, 0, 2), sector + BEFORE]
                cross = (part[3 + s] * cross.astype(F32)).astype(BF16)
                if with_ops(site):
                    right = site_at[slot, s, sector + BEFORE + shift]
                    upper = jnp.concatenate([right, cross], 1)
                    lower = jnp.concatenate([jnp.zeros_like(left), left], 1)
                else:
                    upper, lower = cross, left
                image = jnp.dot(
                    get(site, sector - s), jnp.concatenate([upper, lower], 0), preferred_element_type=F32
                )
                if with_ops(site):
                    image = jnp.concatenate([part[s] * image[:, :BLOCK], image[:, BLOCK:]], 1)
                lefts[sector, s], images[sector, s] = left, image.astype(BF16)
        for sector in sectors:
            total = lax.dot_general(
                jnp.concatenate([lefts[sector, s] for s in range(STATES)], 0),
                jnp.concatenate([images[sector, s] for s in range(STATES)], 0),
                (((0,), (0,)), ((), ())),
                preferred_element_type=F32,
            ).astype(BF16)
            state[site + 1, sector] = total
            for which, index in targets[site + 1, sector]:
                outs[which][index] = total


def run_phase(sites, steps, ins, sources, outs, targets, with_ops, whole, part, mine, other):
    blocks = 15 * sum(len(sectors) for _, sectors in steps)
    return pl.pallas_call(
        functools.partial(phase_kernel, sites, steps, len(ins), sources, targets, with_ops),
        out_shape=[jax.ShapeDtypeStruct(shape, BF16) for shape in outs],
        in_specs=[pl.BlockSpec(memory_space=pltpu.SMEM)] * 2
        + [pl.BlockSpec(memory_space=pl.ANY)] * 2
        + [pl.BlockSpec(memory_space=pltpu.VMEM)] * len(ins),
        out_specs=[pl.BlockSpec(memory_space=pltpu.VMEM)] * len(outs),
        scratch_shapes=[
            pltpu.VMEM((len(sites), STATES, WINDOW, BLOCK, BLOCK), BF16),
            pltpu.SemaphoreType.DMA((len(sites), 2)),
        ],
        compiler_params=pltpu.CompilerParams(vmem_limit_bytes=32 * 1024 * 1024),
        cost_estimate=pl.CostEstimate(flops=blocks * 2 * BLOCK**3, bytes_accessed=4 << 20, transcendentals=0),
    )(whole, part, mine, other, *ins)


def take_piece(start, site, piece, taken, sems):
    first = pl.multiple_of(start[0] * BLOCK, BLOCK)
    spots = [(s, sector * BLOCK) for s in range(STATES) for sector in range(HALF)]
    inward = [
        pltpu.make_async_copy(
            site.at[0, s, pl.ds(first + row, BLOCK)], taken.at[s, pl.ds(row, BLOCK)], sems.at[0, number]
        )
        for number, (s, row) in enumerate(spots)
    ]
    outward = [
        pltpu.make_async_copy(
            taken.at[s, pl.ds(row, BLOCK)], piece.at[s, pl.ds(row, BLOCK)], sems.at[1, number]
        )
        for number, (s, row) in enumerate(spots)
    ]
    for copy in inward:
        copy.start()
    for before, after in zip(inward, outward):
        before.wait()
        after.start()
    for copy in outward:
        copy.wait()


def bring(blocks, held, sem):
    copy = pltpu.make_async_copy(blocks, held, sem)
    copy.start()
    copy.wait()


def add_cores(over, summed):
    for site in range(4):
        both = (over[0, site].astype(F32) + over[1, site].astype(F32)).astype(BF16)
        for piece in range(8):
            summed[site, piece % 2, piece // 2] = both[piece]


def add_columns(over, summed):
    total = over[0].astype(F32)
    for source in range(1, 32):
        total += over[source].astype(F32)
    summed[...] = total.astype(BF16)


def add_up(kernel, array, out):
    return pl.pallas_call(
        kernel,
        out_shape=jax.ShapeDtypeStruct(out, BF16),
        in_specs=[pl.BlockSpec(memory_space=pltpu.VMEM)],
        out_specs=pl.BlockSpec(memory_space=pltpu.VMEM),
        compiler_params=pltpu.CompilerParams(vmem_limit_bytes=16 << 20),
        cost_estimate=pl.CostEstimate(flops=1 << 19, bytes_accessed=2 << 20, transcendentals=0),
    )(array)


def body(site_tensor, term_ops, env_rows, term_shift, keep_weight, env_weight):
    sectors = site_tensor.shape[2] // BLOCK
    core = lax.axis_index("core")
    at_zlo, at_yl, at_y0 = (lax.axis_index(name) for name in ("zlo", "yl", "y0"))
    group = lax.axis_index("x") * 2 + at_y0

    start = site_start(sectors, group, at_zlo).astype(jnp.int32).reshape(1)
    piece = pl.pallas_call(
        take_piece,
        out_shape=jax.ShapeDtypeStruct((STATES, HALF * BLOCK, BLOCK), BF16),
        in_specs=[pl.BlockSpec(memory_space=pltpu.SMEM), pl.BlockSpec(memory_space=pltpu.HBM)],
        out_specs=pl.BlockSpec(memory_space=pltpu.HBM),
        scratch_shapes=[pltpu.VMEM((STATES, HALF * BLOCK, BLOCK), BF16), pltpu.SemaphoreType.DMA((2, STATES * HALF))],
        compiler_params=pltpu.CompilerParams(vmem_limit_bytes=60 << 20),
        cost_estimate=pl.CostEstimate(flops=0, bytes_accessed=800_000, transcendentals=0),
    )(start, site_tensor).reshape(STATES, HALF, BLOCK, BLOCK)
    mine = lax.all_gather(piece, ("zhi", "zlo"))
    spots = [site_start(sectors, group, half) - (OWN * group - BEFORE) for half in range(2)]

    pieces = ops_pieces(term_ops[0].reshape(sectors, BLOCK, BLOCK), term_shift[0], core)
    over = lax.all_to_all(pieces, "x", 0, 0)
    ops_now = lax.dynamic_index_in_dim(over, lax.axis_index("zhi"), 0, keepdims=False)
    ops_now = lax.ppermute(ops_now, ("core", "y0"), [(0, 0), (1, 2), (2, 1), (3, 3)])
    figures = jnp.concatenate([keep_weight[0], env_weight[0], term_shift.astype(F32), jnp.zeros((1,), F32)])
    figures = lax.ppermute(figures, AXES, to_groups())
    shift = figures[6].astype(jnp.int32)
    partner = jnp.arange(STATES, dtype=jnp.int32) - shift
    factors = jnp.where((partner >= 0) & (partner <= 2), figures[3:6], 0.0)
    part = jnp.concatenate([figures[:3], factors])
    whole = jnp.stack([core, shift] + spots).astype(jnp.int32)

    piece = lax.ppermute(env_rows, AXES, rows_to_groups(0))
    halo = lax.ppermute(env_rows, AXES, rows_to_groups(1))
    env_now = jnp.zeros((2 * OWN * BLOCK, BLOCK), BF16)
    spot = at_yl * BLOCK + core * (BLOCK // 2)
    env_now = lax.dynamic_update_slice_in_dim(env_now, halo, spot, 0)
    env_now = lax.dynamic_update_slice_in_dim(env_now, piece, spot + OWN * BLOCK, 0)
    window = jnp.concatenate([ops_now, env_now.reshape(2 * OWN, BLOCK, BLOCK)], 2)

    mine, window, whole, part = lax.optimization_barrier((mine, window, whole, part))
    other = lax.ppermute(mine, "core", [(0, 1), (1, 0)])
    mine = pl.pallas_call(
        bring,
        out_shape=jax.ShapeDtypeStruct(mine.shape, BF16),
        in_specs=[pl.BlockSpec(memory_space=pl.ANY)],
        out_specs=pl.BlockSpec(memory_space=pltpu.VMEM),
        scratch_shapes=[pltpu.SemaphoreType.DMA],
        compiler_params=pltpu.CompilerParams(vmem_limit_bytes=16 << 20),
        cost_estimate=pl.CostEstimate(flops=0, bytes_accessed=6 << 20, transcendentals=0),
    )(mine)

    wide = (BLOCK, 2 * BLOCK)
    onward = [(i, i + 1) for i in range(7)]

    def before_last(site):
        return site < 7

    sources = {(0, sector): (0, sector + OWN) for sector in range(-OWN, OWN)}
    targets = {(1, -2): [], (1, -1): []}
    for sector in range(OWN):
        targets[1, sector] = [(0, sector)]
        targets[2, sector] = [(1, sector)] + ([(3, (0, sector - 2))] if sector >= 2 else [])
    for sector in (2, 3):
        targets[3, sector] = [(2, sector - 2), (3, (1, sector - 2))]
    first, full, upper, tails = run_phase(
        [0, 1, 2],
        [(0, range(-2, OWN)), (1, range(OWN)), (2, (2, 3))],
        [window],
        sources,
        [(OWN,) + wide, (OWN,) + wide, (2,) + wide, (2, 2) + wide],
        targets,
        before_last,
        whole,
        part,
        mine,
        other,
    )
    bonds = [first[:, :, BLOCK:], full[:, :, BLOCK:]]
    for site in (2, 4, 6):
        tails = lax.ppermute(tails, ("x", "y0"), onward)
        last = site == 6
        sources = {}
        for sector in (-2, -1):
            sources[site, sector] = (2, (0, sector + 2))
            sources[site + 1, sector] = (2, (1, sector + 2))
        for sector in range(OWN):
            sources[site, sector] = (0, sector)
        for sector in (2, 3):
            sources[site + 1, sector] = (1, sector - 2)
        targets = {}
        for sector in (0, 1):
            targets[site + 1, sector] = [(0, sector)]
        for sector in range(OWN):
            targets[site + 2, sector] = [(1, sector)]
        steps = [(site, (0, 1)), (site + 1, range(OWN))]
        outs = [(2,) + wide, (OWN,) + ((BLOCK, BLOCK) if last else wide)]
        if not last:
            for sector in (2, 3):
                targets[site + 2, sector].append((3, (0, sector - 2)))
                targets[site + 3, sector] = [(2, sector - 2), (3, (1, sector - 2))]
            steps.append((site + 2, (2, 3)))
            outs += [(2,) + wide, (2, 2) + wide]
        old_upper = upper
        lower, full, *rest = run_phase(
            [site, site + 1] + ([] if last else [site + 2]),
            steps,
            [full, upper, tails],
            sources,
            outs,
            targets,
            before_last,
            whole,
            part,
            mine,
            other,
        )
        bonds += [lower[:, :, BLOCK:], old_upper[:, :, BLOCK:], full if last else full[:, :, BLOCK:]]
        if not last:
            upper, tails = rest

    partial = jnp.concatenate(bonds, 0).reshape(4, 2, 8, BLOCK // 2, BLOCK).transpose(1, 0, 2, 3, 4)
    over = lax.all_to_all(partial, "core", 0, 0)
    summed = add_up(add_cores, over, (4, 2, 4, BLOCK // 2, BLOCK)).reshape(32, BLOCK // 2, BLOCK)
    over = lax.all_to_all(summed, ("zhi", "zlo", "yl"), 0, 0)
    summed = add_up(add_columns, over, (BLOCK // 2, BLOCK))
    swapped = lax.ppermute(summed, ("zlo", "y0"), SWAP)
    return jnp.where(at_zlo == at_y0, summed, swapped)[None]


def solution(mesh):
    parts = Mesh(mesh.devices.reshape(4, 2, 4, 2, 4, 2), AXES)
    seg, op = ("zhi", "core"), ("x", "zlo", "yl", "y0")
    placed = (P(seg, None, None, None), P(op, None, None), P(op, None), P(op), P(op, None), P(op, None))
    return jax.shard_map(body, mesh=parts, in_specs=placed, out_specs=P(seg, op, None), check_vma=False)
```

```python
import functools
import itertools

import jax
import jax.numpy as jnp
from jax import lax
from jax.experimental import pallas as pl
from jax.experimental.pallas import tpu as pltpu
from jax.sharding import Mesh, PartitionSpec as P

BLOCK = 128
OWN = 4
HALF = 4
WINDOW = 2 * HALF
BEFORE = 3
RING = 8
STATES = 3
AXES = ("zhi", "core", "x", "zlo", "yl", "y0")
BF16 = jnp.bfloat16
F32 = jnp.float32


def device_number(zhi, core, x, zlo, yl, y0):
    return ((((zhi * 2 + core) * 4 + x) * 2 + zlo) * 4 + yl) * 2 + y0


def all_places():
    return itertools.product(range(4), range(2), range(4), range(2), range(4), range(2))


def to_groups():
    return [
        (device_number(zhi, core, x, zlo, yl, y0), device_number(x, y0, zhi, zlo, yl, core))
        for zhi, core, x, zlo, yl, y0 in all_places()
    ]


def rows_to_groups(halo):
    pairs = []
    for zhi, core, x, zlo, yl, y0 in all_places():
        group = 2 * x + zlo + halo
        if zhi == 0 and core == y0 and group < 8:
            target = device_number(0, core, group // 2, zlo, yl, group % 2)
            pairs.append((device_number(0, core, x, zlo, yl, y0), target))
    return pairs


SWAP = [(1, 2), (2, 1)]


def site_start(sectors, slice_at, half):
    return jnp.clip(OWN * slice_at - BEFORE + HALF * half, 0, sectors - HALF)


def ops_pieces(ops_blocks, shift, core):
    sectors = ops_blocks.shape[0]
    target = jnp.arange(sectors, dtype=jnp.int32) + shift
    inside = (target >= 0) & (target < sectors)
    masked = jnp.where(inside[:, None, None], ops_blocks, jnp.zeros((), BF16))
    lower = jnp.concatenate([jnp.zeros_like(masked[:OWN]), masked[:-OWN]], 0)
    return jnp.where(core == 0, lower, masked).reshape(4, 2 * OWN, BLOCK, BLOCK)


def phase_kernel(sites, steps, n_in, sources, targets, with_ops, *refs):
    whole, part, mine, other = refs[:4]
    ins = refs[4 : 4 + n_in]
    outs = refs[4 + n_in : -2]
    site_at, sems = refs[-2:]
    core = whole[0]
    shift = whole[1]

    def copies(slot, site, source):
        return [
            pltpu.make_async_copy(
                source.at[(site // 2) * 2 + half],
                site_at.at[slot, :, pl.ds(whole[2 + half], HALF)],
                sems.at[slot, half],
            )
            for half in range(2)
        ]

    @pl.when(whole[2] != 0)
    def _():
        site_at[:, :, :BEFORE] = jnp.zeros((len(sites), STATES, BEFORE, BLOCK, BLOCK), BF16)

    @pl.when(whole[3] != HALF)
    def _():
        site_at[:, :, WINDOW - 1] = jnp.zeros((len(sites), STATES, BLOCK, BLOCK), BF16)

    for slot, site in enumerate(sites):
        @pl.when(core == site % 2)
        def _():
            for copy in copies(slot, site, mine):
                copy.start()

        @pl.when(core != site % 2)
        def _():
            for copy in copies(slot, site, other):
                copy.start()

    state = {}

    def get(site, sector):
        if (site, sector) in state:
            return state[site, sector]
        where, index = sources[site, sector]
        return ins[where][index]

    for site, sectors in steps:
        slot = sites.index(site)
        for copy in copies(slot, site, mine):
            copy.wait()
        lefts, images = {}, {}
        for sector in sectors:
            for s in range(STATES):
                left = site_at[slot, s, sector + BEFORE]
                cross = site_at[slot, jnp.clip(s - shift, 0, 2), sector + BEFORE]
                cross = (part[3 + s] * cross.astype(F32)).astype(BF16)
                if with_ops(site):
                    right = site_at[slot, s, sector + BEFORE + shift]
                    upper = jnp.concatenate([right, cross], 1)
                    lower = jnp.concatenate([jnp.zeros_like(left), left], 1)
                else:
                    upper, lower = cross, left
                image = jnp.dot(
                    get(site, sector - s), jnp.concatenate([upper, lower], 0), preferred_element_type=F32
                )
                if with_ops(site):
                    image = jnp.concatenate([part[s] * image[:, :BLOCK], image[:, BLOCK:]], 1)
                lefts[sector, s], images[sector, s] = left, image.astype(BF16)
        for sector in sectors:
            total = lax.dot_general(
                jnp.concatenate([lefts[sector, s] for s in range(STATES)], 0),
                jnp.concatenate([images[sector, s] for s in range(STATES)], 0),
                (((0,), (0,)), ((), ())),
                preferred_element_type=F32,
            ).astype(BF16)
            state[site + 1, sector] = total
            for which, index in targets[site + 1, sector]:
                outs[which][index] = total


def run_phase(sites, steps, ins, sources, outs, targets, with_ops, whole, part, mine, other):
    blocks = 15 * sum(len(sectors) for _, sectors in steps)
    return pl.pallas_call(
        functools.partial(phase_kernel, sites, steps, len(ins), sources, targets, with_ops),
        out_shape=[jax.ShapeDtypeStruct(shape, BF16) for shape in outs],
        in_specs=[pl.BlockSpec(memory_space=pltpu.SMEM)] * 2
        + [pl.BlockSpec(memory_space=pl.ANY)] * 2
        + [pl.BlockSpec(memory_space=pltpu.VMEM)] * len(ins),
        out_specs=[pl.BlockSpec(memory_space=pltpu.VMEM)] * len(outs),
        scratch_shapes=[
            pltpu.VMEM((len(sites), STATES, WINDOW, BLOCK, BLOCK), BF16),
            pltpu.SemaphoreType.DMA((len(sites), 2)),
        ],
        compiler_params=pltpu.CompilerParams(vmem_limit_bytes=32 * 1024 * 1024),
        cost_estimate=pl.CostEstimate(flops=blocks * 2 * BLOCK**3, bytes_accessed=4 << 20, transcendentals=0),
    )(whole, part, mine, other, *ins)


def take_piece(start, site, piece, sems):
    first = pl.multiple_of(start[0] * BLOCK, BLOCK)
    taken = [
        pltpu.make_async_copy(site.at[0, s, pl.ds(first, HALF * BLOCK)], piece.at[s], sems.at[s])
        for s in range(STATES)
    ]
    for copy in taken:
        copy.start()
    for copy in taken:
        copy.wait()


def in_order(steps, place, *refs):
    pieces, held, sems = refs[:-2], refs[-2], refs[-1]
    brought = [
        pltpu.make_async_copy(piece, held.at[lax.rem(place[0] + step + RING, RING)], sems.at[number])
        for number, (step, piece) in enumerate(zip(steps, pieces))
    ]
    for copy in brought:
        copy.start()
    for copy in brought:
        copy.wait()


def gather_along_z(piece, place):
    upward = [(i, (i + 1) % RING) for i in range(RING)]
    downward = [(i, (i - 1) % RING) for i in range(RING)]
    arrived = {0: piece}
    for step in range(1, RING // 2 + 1):
        arrived[-step] = lax.ppermute(arrived[1 - step], ("zhi", "zlo"), upward)
        if step < RING // 2:
            arrived[step] = lax.ppermute(arrived[step - 1], ("zhi", "zlo"), downward)
    return pl.pallas_call(
        functools.partial(in_order, tuple(arrived)),
        out_shape=jax.ShapeDtypeStruct((RING,) + piece.shape, BF16),
        in_specs=[pl.BlockSpec(memory_space=pltpu.SMEM)] + [pl.BlockSpec(memory_space=pl.ANY)] * RING,
        out_specs=pl.BlockSpec(memory_space=pltpu.VMEM),
        scratch_shapes=[pltpu.SemaphoreType.DMA((RING,))],
        compiler_params=pltpu.CompilerParams(vmem_limit_bytes=16 << 20),
        cost_estimate=pl.CostEstimate(flops=0, bytes_accessed=6 << 20, transcendentals=0),
    )(place, *arrived.values())


def add_cores(over, summed):
    for site in range(4):
        both = (over[0, site].astype(F32) + over[1, site].astype(F32)).astype(BF16)
        for piece in range(8):
            summed[site, piece % 2, piece // 2] = both[piece]


def add_columns(over, summed):
    total = over[0].astype(F32)
    for source in range(1, 32):
        total += over[source].astype(F32)
    summed[...] = total.astype(BF16)


def add_up(kernel, array, out):
    return pl.pallas_call(
        kernel,
        out_shape=jax.ShapeDtypeStruct(out, BF16),
        in_specs=[pl.BlockSpec(memory_space=pltpu.VMEM)],
        out_specs=pl.BlockSpec(memory_space=pltpu.VMEM),
        compiler_params=pltpu.CompilerParams(vmem_limit_bytes=16 << 20),
        cost_estimate=pl.CostEstimate(flops=1 << 19, bytes_accessed=2 << 20, transcendentals=0),
    )(array)


def body(site_tensor, term_ops, env_rows, term_shift, keep_weight, env_weight):
    sectors = site_tensor.shape[2] // BLOCK
    core = lax.axis_index("core")
    at_zlo, at_yl, at_y0 = (lax.axis_index(name) for name in ("zlo", "yl", "y0"))
    group = lax.axis_index("x") * 2 + at_y0

    start = site_start(sectors, group, at_zlo).astype(jnp.int32).reshape(1)
    piece = pl.pallas_call(
        take_piece,
        out_shape=jax.ShapeDtypeStruct((STATES, HALF * BLOCK, BLOCK), BF16),
        in_specs=[pl.BlockSpec(memory_space=pltpu.SMEM), pl.BlockSpec(memory_space=pl.ANY)],
        out_specs=pl.BlockSpec(memory_space=pltpu.VMEM),
        scratch_shapes=[pltpu.SemaphoreType.DMA((STATES,))],
        compiler_params=pltpu.CompilerParams(vmem_limit_bytes=60 << 20),
        cost_estimate=pl.CostEstimate(flops=0, bytes_accessed=800_000, transcendentals=0),
    )(start, site_tensor).reshape(STATES, HALF, BLOCK, BLOCK)
    place = (lax.axis_index("zhi") * 2 + at_zlo).astype(jnp.int32).reshape(1)
    mine = gather_along_z(piece, place)
    spots = [site_start(sectors, group, half) - (OWN * group - BEFORE) for half in range(2)]

    pieces = ops_pieces(term_ops[0].reshape(sectors, BLOCK, BLOCK), term_shift[0], core)
    over = lax.all_to_all(pieces, "x", 0, 0)
    ops_now = lax.dynamic_index_in_dim(over, lax.axis_index("zhi"), 0, keepdims=False)
    ops_now = lax.ppermute(ops_now, ("core", "y0"), [(0, 0), (1, 2), (2, 1), (3, 3)])
    figures = jnp.concatenate([keep_weight[0], env_weight[0], term_shift.astype(F32), jnp.zeros((1,), F32)])
    figures = lax.ppermute(figures, AXES, to_groups())
    shift = figures[6].astype(jnp.int32)
    partner = jnp.arange(STATES, dtype=jnp.int32) - shift
    factors = jnp.where((partner >= 0) & (partner <= 2), figures[3:6], 0.0)
    part = jnp.concatenate([figures[:3], factors])
    whole = jnp.stack([core, shift] + spots).astype(jnp.int32)

    piece = lax.ppermute(env_rows, AXES, rows_to_groups(0))
    halo = lax.ppermute(env_rows, AXES, rows_to_groups(1))
    env_now = jnp.zeros((2 * OWN * BLOCK, BLOCK), BF16)
    spot = at_yl * BLOCK + core * (BLOCK // 2)
    env_now = lax.dynamic_update_slice_in_dim(env_now, halo, spot, 0)
    env_now = lax.dynamic_update_slice_in_dim(env_now, piece, spot + OWN * BLOCK, 0)
    window = jnp.concatenate([ops_now, env_now.reshape(2 * OWN, BLOCK, BLOCK)], 2)

    mine, window, whole, part = lax.optimization_barrier((mine, window, whole, part))
    other = lax.ppermute(mine, "core", [(0, 1), (1, 0)])

    wide = (BLOCK, 2 * BLOCK)
    onward = [(i, i + 1) for i in range(7)]

    def before_last(site):
        return site < 7

    sources = {(0, sector): (0, sector + OWN) for sector in range(-OWN, OWN)}
    targets = {(1, -2): [], (1, -1): []}
    for sector in range(OWN):
        targets[1, sector] = [(0, sector)]
        targets[2, sector] = [(1, sector)] + ([(3, (0, sector - 2))] if sector >= 2 else [])
    for sector in (2, 3):
        targets[3, sector] = [(2, sector - 2), (3, (1, sector - 2))]
    first, full, upper, tails = run_phase(
        [0, 1, 2],
        [(0, range(-2, OWN)), (1, range(OWN)), (2, (2, 3))],
        [window],
        sources,
        [(OWN,) + wide, (OWN,) + wide, (2,) + wide, (2, 2) + wide],
        targets,
        before_last,
        whole,
        part,
        mine,
        other,
    )
    bonds = [first[:, :, BLOCK:], full[:, :, BLOCK:]]
    for site in (2, 4, 6):
        tails = lax.ppermute(tails, ("x", "y0"), onward)
        last = site == 6
        sources = {}
        for sector in (-2, -1):
            sources[site, sector] = (2, (0, sector + 2))
            sources[site + 1, sector] = (2, (1, sector + 2))
        for sector in range(OWN):
            sources[site, sector] = (0, sector)
        for sector in (2, 3):
            sources[site + 1, sector] = (1, sector - 2)
        targets = {}
        for sector in (0, 1):
            targets[site + 1, sector] = [(0, sector)]
        for sector in range(OWN):
            targets[site + 2, sector] = [(1, sector)]
        steps = [(site, (0, 1)), (site + 1, range(OWN))]
        outs = [(2,) + wide, (OWN,) + ((BLOCK, BLOCK) if last else wide)]
        if not last:
            for sector in (2, 3):
                targets[site + 2, sector].append((3, (0, sector - 2)))
                targets[site + 3, sector] = [(2, sector - 2), (3, (1, sector - 2))]
            steps.append((site + 2, (2, 3)))
            outs += [(2,) + wide, (2, 2) + wide]
        old_upper = upper
        lower, full, *rest = run_phase(
            [site, site + 1] + ([] if last else [site + 2]),
            steps,
            [full, upper, tails],
            sources,
            outs,
            targets,
            before_last,
            whole,
            part,
            mine,
            other,
        )
        bonds += [lower[:, :, BLOCK:], old_upper[:, :, BLOCK:], full if last else full[:, :, BLOCK:]]
        if not last:
            upper, tails = rest

    partial = jnp.concatenate(bonds, 0).reshape(4, 2, 8, BLOCK // 2, BLOCK).transpose(1, 0, 2, 3, 4)
    over = lax.all_to_all(partial, "core", 0, 0)
    summed = add_up(add_cores, over, (4, 2, 4, BLOCK // 2, BLOCK)).reshape(32, BLOCK // 2, BLOCK)
    over = lax.all_to_all(summed, ("zhi", "zlo", "yl"), 0, 0)
    summed = add_up(add_columns, over, (BLOCK // 2, BLOCK))
    swapped = lax.ppermute(summed, ("zlo", "y0"), SWAP)
    return jnp.where(at_zlo == at_y0, summed, swapped)[None]


def solution(mesh):
    parts = Mesh(mesh.devices.reshape(4, 2, 4, 2, 4, 2), AXES)
    seg, op = ("zhi", "core"), ("x", "zlo", "yl", "y0")
    placed = (P(seg, None, None, None), P(op, None, None), P(op, None), P(op), P(op, None), P(op, None))
    return jax.shard_map(body, mesh=parts, in_specs=placed, out_specs=P(seg, op, None), check_vma=False)
```

```python
import functools
import itertools

import jax
import jax.numpy as jnp
from jax import lax
from jax.experimental import pallas as pl
from jax.experimental.pallas import tpu as pltpu
from jax.sharding import Mesh, PartitionSpec as P

BLOCK = 128
OWN = 4
HALF = 4
WINDOW = 2 * HALF
BEFORE = 3
RING = 8
STATES = 3
AXES = ("zhi", "core", "x", "zlo", "yl", "y0")
BF16 = jnp.bfloat16
F32 = jnp.float32


def device_number(zhi, core, x, zlo, yl, y0):
    return ((((zhi * 2 + core) * 4 + x) * 2 + zlo) * 4 + yl) * 2 + y0


def all_places():
    return itertools.product(range(4), range(2), range(4), range(2), range(4), range(2))


def to_groups():
    return [
        (device_number(zhi, core, x, zlo, yl, y0), device_number(x, y0, zhi, zlo, yl, core))
        for zhi, core, x, zlo, yl, y0 in all_places()
    ]


def rows_to_groups(halo):
    pairs = []
    for zhi, core, x, zlo, yl, y0 in all_places():
        group = 2 * x + zlo + halo
        if zhi == 0 and core == y0 and group < 8:
            target = device_number(0, core, group // 2, zlo, yl, group % 2)
            pairs.append((device_number(0, core, x, zlo, yl, y0), target))
    return pairs


SWAP = [(1, 2), (2, 1)]


def site_start(sectors, slice_at, half):
    return jnp.clip(OWN * slice_at - BEFORE + HALF * half, 0, sectors - HALF)


def ops_pieces(ops_blocks, shift, core):
    sectors = ops_blocks.shape[0]
    target = jnp.arange(sectors, dtype=jnp.int32) + shift
    inside = (target >= 0) & (target < sectors)
    masked = jnp.where(inside[:, None, None], ops_blocks, jnp.zeros((), BF16))
    lower = jnp.concatenate([jnp.zeros_like(masked[:OWN]), masked[:-OWN]], 0)
    return jnp.where(core == 0, lower, masked).reshape(4, 2 * OWN, BLOCK, BLOCK)


def phase_kernel(sites, steps, n_in, sources, targets, with_ops, *refs):
    whole, part, mine, other = refs[:4]
    ins = refs[4 : 4 + n_in]
    outs = refs[4 + n_in : -2]
    site_at, sems = refs[-2:]
    core = whole[0]
    shift = whole[1]

    def copies(slot, site, source):
        return [
            pltpu.make_async_copy(
                source.at[(site // 2) * 2 + half],
                site_at.at[slot, :, pl.ds(whole[2 + half], HALF)],
                sems.at[slot, half],
            )
            for half in range(2)
        ]

    @pl.when(whole[2] != 0)
    def _():
        site_at[:, :, :BEFORE] = jnp.zeros((len(sites), STATES, BEFORE, BLOCK, BLOCK), BF16)

    @pl.when(whole[3] != HALF)
    def _():
        site_at[:, :, WINDOW - 1] = jnp.zeros((len(sites), STATES, BLOCK, BLOCK), BF16)

    for slot, site in enumerate(sites):
        @pl.when(core == site % 2)
        def _():
            for copy in copies(slot, site, mine):
                copy.start()

        @pl.when(core != site % 2)
        def _():
            for copy in copies(slot, site, other):
                copy.start()

    state = {}

    def get(site, sector):
        if (site, sector) in state:
            return state[site, sector]
        where, index = sources[site, sector]
        return ins[where][index]

    for site, sectors in steps:
        slot = sites.index(site)
        for copy in copies(slot, site, mine):
            copy.wait()
        lefts, images = {}, {}
        for sector in sectors:
            for s in range(STATES):
                left = site_at[slot, s, sector + BEFORE]
                cross = site_at[slot, jnp.clip(s - shift, 0, 2), sector + BEFORE]
                cross = (part[3 + s] * cross.astype(F32)).astype(BF16)
                if with_ops(site):
                    right = site_at[slot, s, sector + BEFORE + shift]
                    upper = jnp.concatenate([right, cross], 1)
                    lower = jnp.concatenate([jnp.zeros_like(left), left], 1)
                else:
                    upper, lower = cross, left
                image = jnp.dot(
                    get(site, sector - s), jnp.concatenate([upper, lower], 0), preferred_element_type=F32
                )
                if with_ops(site):
                    image = jnp.concatenate([part[s] * image[:, :BLOCK], image[:, BLOCK:]], 1)
                lefts[sector, s], images[sector, s] = left, image.astype(BF16)
        for sector in sectors:
            total = lax.dot_general(
                jnp.concatenate([lefts[sector, s] for s in range(STATES)], 0),
                jnp.concatenate([images[sector, s] for s in range(STATES)], 0),
                (((0,), (0,)), ((), ())),
                preferred_element_type=F32,
            ).astype(BF16)
            state[site + 1, sector] = total
            for which, index in targets[site + 1, sector]:
                outs[which][index] = total


def run_phase(sites, steps, ins, sources, outs, targets, with_ops, whole, part, mine, other):
    blocks = 15 * sum(len(sectors) for _, sectors in steps)
    return pl.pallas_call(
        functools.partial(phase_kernel, sites, steps, len(ins), sources, targets, with_ops),
        out_shape=[jax.ShapeDtypeStruct(shape, BF16) for shape in outs],
        in_specs=[pl.BlockSpec(memory_space=pltpu.SMEM)] * 2
        + [pl.BlockSpec(memory_space=pl.ANY)] * 2
        + [pl.BlockSpec(memory_space=pltpu.VMEM)] * len(ins),
        out_specs=[pl.BlockSpec(memory_space=pltpu.VMEM)] * len(outs),
        scratch_shapes=[
            pltpu.VMEM((len(sites), STATES, WINDOW, BLOCK, BLOCK), BF16),
            pltpu.SemaphoreType.DMA((len(sites), 2)),
        ],
        compiler_params=pltpu.CompilerParams(vmem_limit_bytes=32 * 1024 * 1024),
        cost_estimate=pl.CostEstimate(flops=blocks * 2 * BLOCK**3, bytes_accessed=4 << 20, transcendentals=0),
    )(whole, part, mine, other, *ins)


def take_piece(start, site, piece, sems):
    first = pl.multiple_of(start[0] * BLOCK, BLOCK)
    taken = [
        pltpu.make_async_copy(site.at[0, s, pl.ds(first, HALF * BLOCK)], piece.at[s], sems.at[s])
        for s in range(STATES)
    ]
    for copy in taken:
        copy.start()
    for copy in taken:
        copy.wait()


def in_order(steps, place, *refs):
    pieces, held, sems = refs[:-2], refs[-2], refs[-1]
    brought = [
        pltpu.make_async_copy(piece, held.at[lax.rem(place[0] + step + RING, RING)], sems.at[number])
        for number, (step, piece) in enumerate(zip(steps, pieces))
    ]
    for copy in brought:
        copy.start()
    for copy in brought:
        copy.wait()


def fill_in(place, last_mine, last_other, mine_in, other_in, mine, other, sems):
    brought = []
    for step in range(1 - RING // 2, RING // 2 + 1):
        spot = lax.rem(place[0] + step + RING, RING)
        for number, (last, most, held) in enumerate(((last_mine, mine_in, mine), (last_other, other_in, other))):
            source = last if step == RING // 2 else most.at[spot]
            brought.append(pltpu.make_async_copy(source, held.at[spot], sems.at[number, step + RING // 2 - 1]))
    for copy in brought:
        copy.start()
    for copy in brought:
        copy.wait()


def gather_along_z(piece, place, between):
    upward = [(i, (i + 1) % RING) for i in range(RING)]
    downward = [(i, (i - 1) % RING) for i in range(RING)]
    swap = [(0, 1), (1, 0)]
    arrived = {0: piece}
    rest = None
    for step in range(1, RING // 2):
        up, down = arrived[1 - step], arrived[step - 1]
        if step > 1:
            rest = between[step - 2](rest)
        up = lax.ppermute(up, ("zhi", "zlo"), upward)
        down = lax.ppermute(down, ("zhi", "zlo"), downward)
        arrived[-step], arrived[step], rest = lax.optimization_barrier((up, down, rest))
    last_mine = lax.ppermute(arrived[1 - RING // 2], ("zhi", "zlo"), upward)
    held = jax.ShapeDtypeStruct((RING,) + piece.shape, BF16)
    params = pltpu.CompilerParams(vmem_limit_bytes=16 << 20)
    scalars, vmem = pl.BlockSpec(memory_space=pltpu.SMEM), pl.BlockSpec(memory_space=pltpu.VMEM)
    mine = pl.pallas_call(
        functools.partial(in_order, tuple(arrived)),
        out_shape=held,
        in_specs=[scalars] + [pl.BlockSpec(memory_space=pl.ANY)] * len(arrived),
        out_specs=vmem,
        scratch_shapes=[pltpu.SemaphoreType.DMA((len(arrived),))],
        compiler_params=params,
        cost_estimate=pl.CostEstimate(flops=0, bytes_accessed=6 << 20, transcendentals=0),
    )(place, *arrived.values())
    other = lax.ppermute(mine, "core", swap)
    last_other = lax.ppermute(last_mine, "core", swap)
    mine, other = pl.pallas_call(
        fill_in,
        out_shape=[held, held],
        in_specs=[scalars] + [pl.BlockSpec(memory_space=pl.ANY)] * 4,
        out_specs=[vmem, vmem],
        scratch_shapes=[pltpu.SemaphoreType.DMA((2, RING))],
        compiler_params=params,
        cost_estimate=pl.CostEstimate(flops=0, bytes_accessed=2 << 20, transcendentals=0),
    )(place, last_mine, last_other, mine, other)
    return mine, other, rest


def add_cores(over, summed):
    for site in range(4):
        both = (over[0, site].astype(F32) + over[1, site].astype(F32)).astype(BF16)
        for piece in range(8):
            summed[site, piece % 2, piece // 2] = both[piece]


def add_columns(over, summed):
    total = over[0].astype(F32)
    for source in range(1, 32):
        total += over[source].astype(F32)
    summed[...] = total.astype(BF16)


def add_up(kernel, array, out):
    return pl.pallas_call(
        kernel,
        out_shape=jax.ShapeDtypeStruct(out, BF16),
        in_specs=[pl.BlockSpec(memory_space=pltpu.VMEM)],
        out_specs=pl.BlockSpec(memory_space=pltpu.VMEM),
        compiler_params=pltpu.CompilerParams(vmem_limit_bytes=16 << 20),
        cost_estimate=pl.CostEstimate(flops=1 << 19, bytes_accessed=2 << 20, transcendentals=0),
    )(array)


def body(site_tensor, term_ops, env_rows, term_shift, keep_weight, env_weight):
    sectors = site_tensor.shape[2] // BLOCK
    core = lax.axis_index("core")
    at_zlo, at_yl, at_y0 = (lax.axis_index(name) for name in ("zlo", "yl", "y0"))
    group = lax.axis_index("x") * 2 + at_y0

    start = site_start(sectors, group, at_zlo).astype(jnp.int32).reshape(1)
    piece = pl.pallas_call(
        take_piece,
        out_shape=jax.ShapeDtypeStruct((STATES, HALF * BLOCK, BLOCK), BF16),
        in_specs=[pl.BlockSpec(memory_space=pltpu.SMEM), pl.BlockSpec(memory_space=pl.ANY)],
        out_specs=pl.BlockSpec(memory_space=pltpu.VMEM),
        scratch_shapes=[pltpu.SemaphoreType.DMA((STATES,))],
        compiler_params=pltpu.CompilerParams(vmem_limit_bytes=60 << 20),
        cost_estimate=pl.CostEstimate(flops=0, bytes_accessed=800_000, transcendentals=0),
    )(start, site_tensor).reshape(STATES, HALF, BLOCK, BLOCK)
    place = (lax.axis_index("zhi") * 2 + at_zlo).astype(jnp.int32).reshape(1)
    spots = [site_start(sectors, group, half) - (OWN * group - BEFORE) for half in range(2)]

    def cross_x(_):
        pieces = ops_pieces(term_ops[0].reshape(sectors, BLOCK, BLOCK), term_shift[0], core)
        return lax.all_to_all(pieces, "x", 0, 0)

    def cross_y(over):
        ops_now = lax.dynamic_index_in_dim(over, lax.axis_index("zhi"), 0, keepdims=False)
        ops_now = lax.ppermute(ops_now, ("core", "y0"), [(0, 0), (1, 2), (2, 1), (3, 3)])
        figures = [keep_weight[0], env_weight[0], term_shift.astype(F32), jnp.zeros((1,), F32)]
        figures = lax.ppermute(jnp.concatenate(figures), AXES, to_groups())
        piece = lax.ppermute(env_rows, AXES, rows_to_groups(0))
        halo = lax.ppermute(env_rows, AXES, rows_to_groups(1))
        return ops_now, figures, piece, halo

    mine, other, (ops_now, figures, piece, halo) = gather_along_z(piece, place, [cross_x, cross_y])
    shift = figures[6].astype(jnp.int32)
    partner = jnp.arange(STATES, dtype=jnp.int32) - shift
    factors = jnp.where((partner >= 0) & (partner <= 2), figures[3:6], 0.0)
    part = jnp.concatenate([figures[:3], factors])
    whole = jnp.stack([core, shift] + spots).astype(jnp.int32)

    env_now = jnp.zeros((2 * OWN * BLOCK, BLOCK), BF16)
    spot = at_yl * BLOCK + core * (BLOCK // 2)
    env_now = lax.dynamic_update_slice_in_dim(env_now, halo, spot, 0)
    env_now = lax.dynamic_update_slice_in_dim(env_now, piece, spot + OWN * BLOCK, 0)
    window = jnp.concatenate([ops_now, env_now.reshape(2 * OWN, BLOCK, BLOCK)], 2)

    wide = (BLOCK, 2 * BLOCK)
    onward = [(i, i + 1) for i in range(7)]

    def before_last(site):
        return site < 7

    sources = {(0, sector): (0, sector + OWN) for sector in range(-OWN, OWN)}
    targets = {(1, -2): [], (1, -1): []}
    for sector in range(OWN):
        targets[1, sector] = [(0, sector)]
        targets[2, sector] = [(1, sector)] + ([(3, (0, sector - 2))] if sector >= 2 else [])
    for sector in (2, 3):
        targets[3, sector] = [(2, sector - 2), (3, (1, sector - 2))]
    first, full, upper, tails = run_phase(
        [0, 1, 2],
        [(0, range(-2, OWN)), (1, range(OWN)), (2, (2, 3))],
        [window],
        sources,
        [(OWN,) + wide, (OWN,) + wide, (2,) + wide, (2, 2) + wide],
        targets,
        before_last,
        whole,
        part,
        mine,
        other,
    )
    bonds = [first[:, :, BLOCK:], full[:, :, BLOCK:]]
    for site in (2, 4, 6):
        tails = lax.ppermute(tails, ("x", "y0"), onward)
        last = site == 6
        sources = {}
        for sector in (-2, -1):
            sources[site, sector] = (2, (0, sector + 2))
            sources[site + 1, sector] = (2, (1, sector + 2))
        for sector in range(OWN):
            sources[site, sector] = (0, sector)
        for sector in (2, 3):
            sources[site + 1, sector] = (1, sector - 2)
        targets = {}
        for sector in (0, 1):
            targets[site + 1, sector] = [(0, sector)]
        for sector in range(OWN):
            targets[site + 2, sector] = [(1, sector)]
        steps = [(site, (0, 1)), (site + 1, range(OWN))]
        outs = [(2,) + wide, (OWN,) + ((BLOCK, BLOCK) if last else wide)]
        if not last:
            for sector in (2, 3):
                targets[site + 2, sector].append((3, (0, sector - 2)))
                targets[site + 3, sector] = [(2, sector - 2), (3, (1, sector - 2))]
            steps.append((site + 2, (2, 3)))
            outs += [(2,) + wide, (2, 2) + wide]
        old_upper = upper
        lower, full, *rest = run_phase(
            [site, site + 1] + ([] if last else [site + 2]),
            steps,
            [full, upper, tails],
            sources,
            outs,
            targets,
            before_last,
            whole,
            part,
            mine,
            other,
        )
        bonds += [lower[:, :, BLOCK:], old_upper[:, :, BLOCK:], full if last else full[:, :, BLOCK:]]
        if not last:
            upper, tails = rest

    partial = jnp.concatenate(bonds, 0).reshape(4, 2, 8, BLOCK // 2, BLOCK).transpose(1, 0, 2, 3, 4)
    over = lax.all_to_all(partial, "core", 0, 0)
    summed = add_up(add_cores, over, (4, 2, 4, BLOCK // 2, BLOCK)).reshape(32, BLOCK // 2, BLOCK)
    over = lax.all_to_all(summed, ("zhi", "zlo", "yl"), 0, 0)
    summed = add_up(add_columns, over, (BLOCK // 2, BLOCK))
    swapped = lax.ppermute(summed, ("zlo", "y0"), SWAP)
    return jnp.where(at_zlo == at_y0, summed, swapped)[None]


def solution(mesh):
    parts = Mesh(mesh.devices.reshape(4, 2, 4, 2, 4, 2), AXES)
    seg, op = ("zhi", "core"), ("x", "zlo", "yl", "y0")
    placed = (P(seg, None, None, None), P(op, None, None), P(op, None), P(op), P(op, None), P(op, None))
    return jax.shard_map(body, mesh=parts, in_specs=placed, out_specs=P(seg, op, None), check_vma=False)
```

```python
import functools
import itertools

import jax
import jax.numpy as jnp
from jax import lax
from jax.experimental import pallas as pl
from jax.experimental.pallas import tpu as pltpu
from jax.sharding import Mesh, PartitionSpec as P

BLOCK = 128
OWN = 4
HALF = 4
WINDOW = 2 * HALF
BEFORE = 3
RING = 8
STATES = 3
AXES = ("zhi", "core", "x", "zlo", "yl", "y0")
BF16 = jnp.bfloat16
F32 = jnp.float32


def device_number(zhi, core, x, zlo, yl, y0):
    return ((((zhi * 2 + core) * 4 + x) * 2 + zlo) * 4 + yl) * 2 + y0


def all_places():
    return itertools.product(range(4), range(2), range(4), range(2), range(4), range(2))


def to_groups():
    return [
        (device_number(zhi, core, x, zlo, yl, y0), device_number(x, y0, zhi, zlo, yl, core))
        for zhi, core, x, zlo, yl, y0 in all_places()
    ]


def rows_to_groups(halo):
    pairs = []
    for zhi, core, x, zlo, yl, y0 in all_places():
        group = 2 * x + zlo + halo
        if zhi == 0 and core == y0 and group < 8:
            target = device_number(0, core, group // 2, zlo, yl, group % 2)
            pairs.append((device_number(0, core, x, zlo, yl, y0), target))
    return pairs


SWAP = [(1, 2), (2, 1)]


def site_start(sectors, slice_at, half):
    return jnp.clip(OWN * slice_at - BEFORE + HALF * half, 0, sectors - HALF)


def ops_pieces(ops_blocks, shift, core):
    sectors = ops_blocks.shape[0]
    target = jnp.arange(sectors, dtype=jnp.int32) + shift
    inside = (target >= 0) & (target < sectors)
    masked = jnp.where(inside[:, None, None], ops_blocks, jnp.zeros((), BF16))
    lower = jnp.concatenate([jnp.zeros_like(masked[:OWN]), masked[:-OWN]], 0)
    return jnp.where(core == 0, lower, masked).reshape(4, 2 * OWN, BLOCK, BLOCK)


def phase_kernel(sites, steps, n_in, sources, targets, with_ops, *refs):
    whole, part, mine, other, last_mine, last_other = refs[:6]
    ins = refs[6 : 6 + n_in]
    outs = refs[6 + n_in : -2]
    site_at, sems = refs[-2:]
    core, shift, opposite = whole[0], whole[1], whole[4]

    def copy(slot, half, source):
        return pltpu.make_async_copy(
            source, site_at.at[slot, :, pl.ds(whole[2 + half], HALF)], sems.at[slot, half]
        )

    @pl.when(whole[2] != 0)
    def _():
        site_at[:, :, :BEFORE] = jnp.zeros((len(sites), STATES, BEFORE, BLOCK, BLOCK), BF16)

    @pl.when(whole[3] != HALF)
    def _():
        site_at[:, :, WINDOW - 1] = jnp.zeros((len(sites), STATES, BLOCK, BLOCK), BF16)

    for slot, site in enumerate(sites):
        for half in range(2):
            spot = site // 2 * 2 + half
            for own, held, last in ((True, mine, last_mine), (False, other, last_other)):
                here = (core == site % 2) == own

                @pl.when(here & (opposite != spot))
                def _():
                    copy(slot, half, held.at[spot]).start()

                @pl.when(here & (opposite == spot))
                def _():
                    copy(slot, half, last).start()

    state = {}

    def get(site, sector):
        if (site, sector) in state:
            return state[site, sector]
        where, index = sources[site, sector]
        return ins[where][index]

    for site, sectors in steps:
        slot = sites.index(site)
        for half in range(2):
            copy(slot, half, last_mine).wait()
        lefts, images = {}, {}
        for sector in sectors:
            for s in range(STATES):
                left = site_at[slot, s, sector + BEFORE]
                cross = site_at[slot, jnp.clip(s - shift, 0, 2), sector + BEFORE]
                cross = (part[3 + s] * cross.astype(F32)).astype(BF16)
                if with_ops(site):
                    right = site_at[slot, s, sector + BEFORE + shift]
                    upper = jnp.concatenate([right, cross], 1)
                    lower = jnp.concatenate([jnp.zeros_like(left), left], 1)
                else:
                    upper, lower = cross, left
                image = jnp.dot(
                    get(site, sector - s), jnp.concatenate([upper, lower], 0), preferred_element_type=F32
                )
                if with_ops(site):
                    image = jnp.concatenate([part[s] * image[:, :BLOCK], image[:, BLOCK:]], 1)
                lefts[sector, s], images[sector, s] = left, image.astype(BF16)
        for sector in sectors:
            total = lax.dot_general(
                jnp.concatenate([lefts[sector, s] for s in range(STATES)], 0),
                jnp.concatenate([images[sector, s] for s in range(STATES)], 0),
                (((0,), (0,)), ((), ())),
                preferred_element_type=F32,
            ).astype(BF16)
            state[site + 1, sector] = total
            for which, index in targets[site + 1, sector]:
                outs[which][index] = total


def run_phase(sites, steps, ins, sources, outs, targets, with_ops, whole, part, blocks):
    products = 15 * sum(len(sectors) for _, sectors in steps)
    return pl.pallas_call(
        functools.partial(phase_kernel, sites, steps, len(ins), sources, targets, with_ops),
        out_shape=[jax.ShapeDtypeStruct(shape, BF16) for shape in outs],
        in_specs=[pl.BlockSpec(memory_space=pltpu.SMEM)] * 2
        + [pl.BlockSpec(memory_space=pl.ANY)] * 4
        + [pl.BlockSpec(memory_space=pltpu.VMEM)] * len(ins),
        out_specs=[pl.BlockSpec(memory_space=pltpu.VMEM)] * len(outs),
        scratch_shapes=[
            pltpu.VMEM((len(sites), STATES, WINDOW, BLOCK, BLOCK), BF16),
            pltpu.SemaphoreType.DMA((len(sites), 2)),
        ],
        compiler_params=pltpu.CompilerParams(vmem_limit_bytes=32 * 1024 * 1024),
        cost_estimate=pl.CostEstimate(flops=products * 2 * BLOCK**3, bytes_accessed=4 << 20, transcendentals=0),
    )(whole, part, *blocks, *ins)


def take_piece(start, site, piece, sems):
    first = pl.multiple_of(start[0] * BLOCK, BLOCK)
    taken = [
        pltpu.make_async_copy(site.at[0, s, pl.ds(first, HALF * BLOCK)], piece.at[s], sems.at[s])
        for s in range(STATES)
    ]
    for copy in taken:
        copy.start()
    for copy in taken:
        copy.wait()


def in_order(steps, place, *refs):
    pieces, held, sems = refs[:-2], refs[-2], refs[-1]
    brought = [
        pltpu.make_async_copy(piece, held.at[lax.rem(place[0] + step + RING, RING)], sems.at[number])
        for number, (step, piece) in enumerate(zip(steps, pieces))
    ]
    for copy in brought:
        copy.start()
    for copy in brought:
        copy.wait()


def gather_along_z(piece, place):
    upward = [(i, (i + 1) % RING) for i in range(RING)]
    downward = [(i, (i - 1) % RING) for i in range(RING)]
    arrived = {0: piece}
    for step in range(1, RING // 2 + 1):
        arrived[-step] = lax.ppermute(arrived[1 - step], ("zhi", "zlo"), upward)
        if step < RING // 2:
            arrived[step] = lax.ppermute(arrived[step - 1], ("zhi", "zlo"), downward)
    last = arrived.pop(-RING // 2)
    mine = pl.pallas_call(
        functools.partial(in_order, tuple(arrived)),
        out_shape=jax.ShapeDtypeStruct((RING,) + piece.shape, BF16),
        in_specs=[pl.BlockSpec(memory_space=pltpu.SMEM)] + [pl.BlockSpec(memory_space=pl.ANY)] * len(arrived),
        out_specs=pl.BlockSpec(memory_space=pltpu.VMEM),
        scratch_shapes=[pltpu.SemaphoreType.DMA((len(arrived),))],
        compiler_params=pltpu.CompilerParams(vmem_limit_bytes=16 << 20),
        cost_estimate=pl.CostEstimate(flops=0, bytes_accessed=6 << 20, transcendentals=0),
    )(place, *arrived.values())
    return mine, last


def add_cores(over, summed):
    for site in range(4):
        both = (over[0, site].astype(F32) + over[1, site].astype(F32)).astype(BF16)
        for piece in range(8):
            summed[site, piece % 2, piece // 2] = both[piece]


def add_columns(over, summed):
    total = over[0].astype(F32)
    for source in range(1, 32):
        total += over[source].astype(F32)
    summed[...] = total.astype(BF16)


def add_up(kernel, array, out):
    return pl.pallas_call(
        kernel,
        out_shape=jax.ShapeDtypeStruct(out, BF16),
        in_specs=[pl.BlockSpec(memory_space=pltpu.VMEM)],
        out_specs=pl.BlockSpec(memory_space=pltpu.VMEM),
        compiler_params=pltpu.CompilerParams(vmem_limit_bytes=16 << 20),
        cost_estimate=pl.CostEstimate(flops=1 << 19, bytes_accessed=2 << 20, transcendentals=0),
    )(array)


def body(site_tensor, term_ops, env_rows, term_shift, keep_weight, env_weight):
    sectors = site_tensor.shape[2] // BLOCK
    core = lax.axis_index("core")
    at_zlo, at_yl, at_y0 = (lax.axis_index(name) for name in ("zlo", "yl", "y0"))
    group = lax.axis_index("x") * 2 + at_y0

    start = site_start(sectors, group, at_zlo).astype(jnp.int32).reshape(1)
    piece = pl.pallas_call(
        take_piece,
        out_shape=jax.ShapeDtypeStruct((STATES, HALF * BLOCK, BLOCK), BF16),
        in_specs=[pl.BlockSpec(memory_space=pltpu.SMEM), pl.BlockSpec(memory_space=pl.ANY)],
        out_specs=pl.BlockSpec(memory_space=pltpu.VMEM),
        scratch_shapes=[pltpu.SemaphoreType.DMA((STATES,))],
        compiler_params=pltpu.CompilerParams(vmem_limit_bytes=60 << 20),
        cost_estimate=pl.CostEstimate(flops=0, bytes_accessed=800_000, transcendentals=0),
    )(start, site_tensor).reshape(STATES, HALF, BLOCK, BLOCK)
    place = (lax.axis_index("zhi") * 2 + at_zlo).astype(jnp.int32).reshape(1)
    mine, last = gather_along_z(piece, place)
    spots = [site_start(sectors, group, half) - (OWN * group - BEFORE) for half in range(2)]

    pieces = ops_pieces(term_ops[0].reshape(sectors, BLOCK, BLOCK), term_shift[0], core)
    over = lax.all_to_all(pieces, "x", 0, 0)
    ops_now = lax.dynamic_index_in_dim(over, lax.axis_index("zhi"), 0, keepdims=False)
    ops_now = lax.ppermute(ops_now, ("core", "y0"), [(0, 0), (1, 2), (2, 1), (3, 3)])
    figures = jnp.concatenate([keep_weight[0], env_weight[0], term_shift.astype(F32), jnp.zeros((1,), F32)])
    figures = lax.ppermute(figures, AXES, to_groups())
    shift = figures[6].astype(jnp.int32)
    partner = jnp.arange(STATES, dtype=jnp.int32) - shift
    factors = jnp.where((partner >= 0) & (partner <= 2), figures[3:6], 0.0)
    part = jnp.concatenate([figures[:3], factors])
    opposite = lax.rem(place[0] + RING // 2, RING)
    whole = jnp.stack([core, shift] + spots + [opposite]).astype(jnp.int32)

    piece = lax.ppermute(env_rows, AXES, rows_to_groups(0))
    halo = lax.ppermute(env_rows, AXES, rows_to_groups(1))
    env_now = jnp.zeros((2 * OWN * BLOCK, BLOCK), BF16)
    spot = at_yl * BLOCK + core * (BLOCK // 2)
    env_now = lax.dynamic_update_slice_in_dim(env_now, halo, spot, 0)
    env_now = lax.dynamic_update_slice_in_dim(env_now, piece, spot + OWN * BLOCK, 0)
    window = jnp.concatenate([ops_now, env_now.reshape(2 * OWN, BLOCK, BLOCK)], 2)

    mine, window, whole, part = lax.optimization_barrier((mine, window, whole, part))
    swap = [(0, 1), (1, 0)]
    blocks = [mine, lax.ppermute(mine, "core", swap), last, lax.ppermute(last, "core", swap)]

    wide = (BLOCK, 2 * BLOCK)
    onward = [(i, i + 1) for i in range(7)]

    def before_last(site):
        return site < 7

    sources = {(0, sector): (0, sector + OWN) for sector in range(-OWN, OWN)}
    targets = {(1, -2): [], (1, -1): []}
    for sector in range(OWN):
        targets[1, sector] = [(0, sector)]
        targets[2, sector] = [(1, sector)] + ([(3, (0, sector - 2))] if sector >= 2 else [])
    for sector in (2, 3):
        targets[3, sector] = [(2, sector - 2), (3, (1, sector - 2))]
    first, full, upper, tails = run_phase(
        [0, 1, 2],
        [(0, range(-2, OWN)), (1, range(OWN)), (2, (2, 3))],
        [window],
        sources,
        [(OWN,) + wide, (OWN,) + wide, (2,) + wide, (2, 2) + wide],
        targets,
        before_last,
        whole,
        part,
        blocks,
    )
    bonds = [first[:, :, BLOCK:], full[:, :, BLOCK:]]
    for site in (2, 4, 6):
        tails = lax.ppermute(tails, ("x", "y0"), onward)
        last = site == 6
        sources = {}
        for sector in (-2, -1):
            sources[site, sector] = (2, (0, sector + 2))
            sources[site + 1, sector] = (2, (1, sector + 2))
        for sector in range(OWN):
            sources[site, sector] = (0, sector)
        for sector in (2, 3):
            sources[site + 1, sector] = (1, sector - 2)
        targets = {}
        for sector in (0, 1):
            targets[site + 1, sector] = [(0, sector)]
        for sector in range(OWN):
            targets[site + 2, sector] = [(1, sector)]
        steps = [(site, (0, 1)), (site + 1, range(OWN))]
        outs = [(2,) + wide, (OWN,) + ((BLOCK, BLOCK) if last else wide)]
        if not last:
            for sector in (2, 3):
                targets[site + 2, sector].append((3, (0, sector - 2)))
                targets[site + 3, sector] = [(2, sector - 2), (3, (1, sector - 2))]
            steps.append((site + 2, (2, 3)))
            outs += [(2,) + wide, (2, 2) + wide]
        old_upper = upper
        lower, full, *rest = run_phase(
            [site, site + 1] + ([] if last else [site + 2]),
            steps,
            [full, upper, tails],
            sources,
            outs,
            targets,
            before_last,
            whole,
            part,
            blocks,
        )
        bonds += [lower[:, :, BLOCK:], old_upper[:, :, BLOCK:], full if last else full[:, :, BLOCK:]]
        if not last:
            upper, tails = rest

    partial = jnp.concatenate(bonds, 0).reshape(4, 2, 8, BLOCK // 2, BLOCK).transpose(1, 0, 2, 3, 4)
    over = lax.all_to_all(partial, "core", 0, 0)
    summed = add_up(add_cores, over, (4, 2, 4, BLOCK // 2, BLOCK)).reshape(32, BLOCK // 2, BLOCK)
    over = lax.all_to_all(summed, ("zhi", "zlo", "yl"), 0, 0)
    summed = add_up(add_columns, over, (BLOCK // 2, BLOCK))
    swapped = lax.ppermute(summed, ("zlo", "y0"), SWAP)
    return jnp.where(at_zlo == at_y0, summed, swapped)[None]


def solution(mesh):
    parts = Mesh(mesh.devices.reshape(4, 2, 4, 2, 4, 2), AXES)
    seg, op = ("zhi", "core"), ("x", "zlo", "yl", "y0")
    placed = (P(seg, None, None, None), P(op, None, None), P(op, None), P(op), P(op, None), P(op, None))
    return jax.shard_map(body, mesh=parts, in_specs=placed, out_specs=P(seg, op, None), check_vma=False)
```

```python
import functools
import itertools

import jax
import jax.numpy as jnp
from jax import lax
from jax.experimental import pallas as pl
from jax.experimental.pallas import tpu as pltpu
from jax.sharding import Mesh, PartitionSpec as P

BLOCK = 128
OWN = 4
HALF = 4
WINDOW = 2 * HALF
BEFORE = 3
STATES = 3
AXES = ("zhi", "core", "x", "zlo", "yl", "y0")
BF16 = jnp.bfloat16
F32 = jnp.float32


def device_number(zhi, core, x, zlo, yl, y0):
    return ((((zhi * 2 + core) * 4 + x) * 2 + zlo) * 4 + yl) * 2 + y0


def all_places():
    return itertools.product(range(4), range(2), range(4), range(2), range(4), range(2))


def to_groups():
    return [
        (device_number(zhi, core, x, zlo, yl, y0), device_number(x, y0, zhi, zlo, yl, core))
        for zhi, core, x, zlo, yl, y0 in all_places()
    ]


def rows_to_groups(halo):
    pairs = []
    for zhi, core, x, zlo, yl, y0 in all_places():
        group = 2 * x + zlo + halo
        if zhi == 0 and core == y0 and group < 8:
            target = device_number(0, core, group // 2, zlo, yl, group % 2)
            pairs.append((device_number(0, core, x, zlo, yl, y0), target))
    return pairs


SWAP = [(1, 2), (2, 1)]


def site_start(sectors, slice_at, half):
    return jnp.clip(OWN * slice_at - BEFORE + HALF * half, 0, sectors - HALF)


def ops_pieces(ops_blocks, shift, core):
    sectors = ops_blocks.shape[0]
    target = jnp.arange(sectors, dtype=jnp.int32) + shift
    inside = (target >= 0) & (target < sectors)
    masked = jnp.where(inside[:, None, None], ops_blocks, jnp.zeros((), BF16))
    lower = jnp.concatenate([jnp.zeros_like(masked[:OWN]), masked[:-OWN]], 0)
    return jnp.where(core == 0, lower, masked).reshape(4, 2 * OWN, BLOCK, BLOCK)


def phase_kernel(sites, steps, n_in, sources, targets, with_ops, *refs):
    whole, part, mine, other = refs[:4]
    ins = refs[4 : 4 + n_in]
    outs = refs[4 + n_in : -2]
    site_at, sems = refs[-2:]
    core = whole[0]
    shift = whole[1]

    def copies(slot, site, source):
        return [
            pltpu.make_async_copy(
                source.at[(site // 2) * 2 + half],
                site_at.at[slot, :, pl.ds(whole[2 + half], HALF)],
                sems.at[slot, half],
            )
            for half in range(2)
        ]

    @pl.when(whole[2] != 0)
    def _():
        site_at[:, :, :BEFORE] = jnp.zeros((len(sites), STATES, BEFORE, BLOCK, BLOCK), BF16)

    @pl.when(whole[3] != HALF)
    def _():
        site_at[:, :, WINDOW - 1] = jnp.zeros((len(sites), STATES, BLOCK, BLOCK), BF16)

    for slot, site in enumerate(sites):
        @pl.when(core == site % 2)
        def _():
            for copy in copies(slot, site, mine):
                copy.start()

        @pl.when(core != site % 2)
        def _():
            for copy in copies(slot, site, other):
                copy.start()

    state = {}

    def get(site, sector):
        if (site, sector) in state:
            return state[site, sector]
        where, index = sources[site, sector]
        return ins[where][index]

    for site, sectors in steps:
        slot = sites.index(site)
        for copy in copies(slot, site, mine):
            copy.wait()
        lefts, images = {}, {}
        for sector in sectors:
            for s in range(STATES):
                left = site_at[slot, s, sector + BEFORE]
                cross = site_at[slot, jnp.clip(s - shift, 0, 2), sector + BEFORE]
                cross = (part[3 + s] * cross.astype(F32)).astype(BF16)
                if with_ops(site):
                    right = site_at[slot, s, sector + BEFORE + shift]
                    upper = jnp.concatenate([right, cross], 1)
                    lower = jnp.concatenate([jnp.zeros_like(left), left], 1)
                else:
                    upper, lower = cross, left
                image = jnp.dot(
                    get(site, sector - s), jnp.concatenate([upper, lower], 0), preferred_element_type=F32
                )
                if with_ops(site):
                    image = jnp.concatenate([part[s] * image[:, :BLOCK], image[:, BLOCK:]], 1)
                lefts[sector, s], images[sector, s] = left, image.astype(BF16)
        for sector in sectors:
            total = lax.dot_general(
                jnp.concatenate([lefts[sector, s] for s in range(STATES)], 0),
                jnp.concatenate([images[sector, s] for s in range(STATES)], 0),
                (((0,), (0,)), ((), ())),
                preferred_element_type=F32,
            ).astype(BF16)
            state[site + 1, sector] = total
            for which, index in targets[site + 1, sector]:
                outs[which][index] = total


def run_phase(sites, steps, ins, sources, outs, targets, with_ops, whole, part, mine, other):
    blocks = 15 * sum(len(sectors) for _, sectors in steps)
    return pl.pallas_call(
        functools.partial(phase_kernel, sites, steps, len(ins), sources, targets, with_ops),
        out_shape=[jax.ShapeDtypeStruct(shape, BF16) for shape in outs],
        in_specs=[pl.BlockSpec(memory_space=pltpu.SMEM)] * 2
        + [pl.BlockSpec(memory_space=pl.ANY)] * 2
        + [pl.BlockSpec(memory_space=pltpu.VMEM)] * len(ins),
        out_specs=[pl.BlockSpec(memory_space=pltpu.VMEM)] * len(outs),
        scratch_shapes=[
            pltpu.VMEM((len(sites), STATES, WINDOW, BLOCK, BLOCK), BF16),
            pltpu.SemaphoreType.DMA((len(sites), 2)),
        ],
        compiler_params=pltpu.CompilerParams(vmem_limit_bytes=32 * 1024 * 1024),
        cost_estimate=pl.CostEstimate(flops=blocks * 2 * BLOCK**3, bytes_accessed=4 << 20, transcendentals=0),
    )(whole, part, mine, other, *ins)


def take_piece(start, site, piece, taken, sems):
    first = pl.multiple_of(start[0] * BLOCK, BLOCK)
    spots = [(s, sector * BLOCK) for s in range(STATES) for sector in range(HALF)]
    inward = [
        pltpu.make_async_copy(
            site.at[0, s, pl.ds(first + row, BLOCK)], taken.at[s, pl.ds(row, BLOCK)], sems.at[0, number]
        )
        for number, (s, row) in enumerate(spots)
    ]
    outward = [
        pltpu.make_async_copy(
            taken.at[s, pl.ds(row, BLOCK)], piece.at[s, pl.ds(row, BLOCK)], sems.at[1, number]
        )
        for number, (s, row) in enumerate(spots)
    ]
    for copy in inward:
        copy.start()
    for before, after in zip(inward, outward):
        before.wait()
        after.start()
    for copy in outward:
        copy.wait()


def bring(blocks, held, sem):
    copy = pltpu.make_async_copy(blocks, held, sem)
    copy.start()
    copy.wait()


def core_exchange(bonds):
    partial = jnp.concatenate(bonds, 0).reshape(-1, 2, 8, BLOCK // 2, BLOCK).swapaxes(0, 1)
    return lax.all_to_all(partial, "core", 0, 0)


def add_cores(early, late, summed):
    for site in range(4):
        pair = [early[core, site] if site < 3 else late[core, 0] for core in range(2)]
        both = (pair[0].astype(F32) + pair[1].astype(F32)).astype(BF16)
        for piece in range(8):
            summed[site, piece % 2, piece // 2] = both[piece]


def add_columns(over, summed):
    total = over[0].astype(F32)
    for source in range(1, 32):
        total += over[source].astype(F32)
    summed[...] = total.astype(BF16)


def add_up(kernel, out, *arrays):
    return pl.pallas_call(
        kernel,
        out_shape=jax.ShapeDtypeStruct(out, BF16),
        in_specs=[pl.BlockSpec(memory_space=pltpu.VMEM)] * len(arrays),
        out_specs=pl.BlockSpec(memory_space=pltpu.VMEM),
        compiler_params=pltpu.CompilerParams(vmem_limit_bytes=16 << 20),
        cost_estimate=pl.CostEstimate(flops=1 << 19, bytes_accessed=2 << 20, transcendentals=0),
    )(*arrays)


def body(site_tensor, term_ops, env_rows, term_shift, keep_weight, env_weight):
    sectors = site_tensor.shape[2] // BLOCK
    core = lax.axis_index("core")
    at_zlo, at_yl, at_y0 = (lax.axis_index(name) for name in ("zlo", "yl", "y0"))
    group = lax.axis_index("x") * 2 + at_y0

    start = site_start(sectors, group, at_zlo).astype(jnp.int32).reshape(1)
    piece = pl.pallas_call(
        take_piece,
        out_shape=jax.ShapeDtypeStruct((STATES, HALF * BLOCK, BLOCK), BF16),
        in_specs=[pl.BlockSpec(memory_space=pltpu.SMEM), pl.BlockSpec(memory_space=pltpu.HBM)],
        out_specs=pl.BlockSpec(memory_space=pltpu.HBM),
        scratch_shapes=[pltpu.VMEM((STATES, HALF * BLOCK, BLOCK), BF16), pltpu.SemaphoreType.DMA((2, STATES * HALF))],
        compiler_params=pltpu.CompilerParams(vmem_limit_bytes=60 << 20),
        cost_estimate=pl.CostEstimate(flops=0, bytes_accessed=800_000, transcendentals=0),
    )(start, site_tensor).reshape(STATES, HALF, BLOCK, BLOCK)
    mine = lax.all_gather(piece, ("zhi", "zlo"))
    spots = [site_start(sectors, group, half) - (OWN * group - BEFORE) for half in range(2)]

    pieces = ops_pieces(term_ops[0].reshape(sectors, BLOCK, BLOCK), term_shift[0], core)
    over = lax.all_to_all(pieces, "x", 0, 0)
    ops_now = lax.dynamic_index_in_dim(over, lax.axis_index("zhi"), 0, keepdims=False)
    ops_now = lax.ppermute(ops_now, ("core", "y0"), [(0, 0), (1, 2), (2, 1), (3, 3)])
    figures = jnp.concatenate([keep_weight[0], env_weight[0], term_shift.astype(F32), jnp.zeros((1,), F32)])
    figures = lax.ppermute(figures, AXES, to_groups())
    shift = figures[6].astype(jnp.int32)
    partner = jnp.arange(STATES, dtype=jnp.int32) - shift
    factors = jnp.where((partner >= 0) & (partner <= 2), figures[3:6], 0.0)
    part = jnp.concatenate([figures[:3], factors])
    whole = jnp.stack([core, shift] + spots).astype(jnp.int32)

    piece = lax.ppermute(env_rows, AXES, rows_to_groups(0))
    halo = lax.ppermute(env_rows, AXES, rows_to_groups(1))
    env_now = jnp.zeros((2 * OWN * BLOCK, BLOCK), BF16)
    spot = at_yl * BLOCK + core * (BLOCK // 2)
    env_now = lax.dynamic_update_slice_in_dim(env_now, halo, spot, 0)
    env_now = lax.dynamic_update_slice_in_dim(env_now, piece, spot + OWN * BLOCK, 0)
    window = jnp.concatenate([ops_now, env_now.reshape(2 * OWN, BLOCK, BLOCK)], 2)

    mine, window, whole, part = lax.optimization_barrier((mine, window, whole, part))
    other = lax.ppermute(mine, "core", [(0, 1), (1, 0)])
    mine = pl.pallas_call(
        bring,
        out_shape=jax.ShapeDtypeStruct(mine.shape, BF16),
        in_specs=[pl.BlockSpec(memory_space=pl.ANY)],
        out_specs=pl.BlockSpec(memory_space=pltpu.VMEM),
        scratch_shapes=[pltpu.SemaphoreType.DMA],
        compiler_params=pltpu.CompilerParams(vmem_limit_bytes=16 << 20),
        cost_estimate=pl.CostEstimate(flops=0, bytes_accessed=6 << 20, transcendentals=0),
    )(mine)

    wide = (BLOCK, 2 * BLOCK)
    onward = [(i, i + 1) for i in range(7)]

    def before_last(site):
        return site < 7

    sources = {(0, sector): (0, sector + OWN) for sector in range(-OWN, OWN)}
    targets = {(1, -2): [], (1, -1): []}
    for sector in range(OWN):
        targets[1, sector] = [(0, sector)]
        targets[2, sector] = [(1, sector)] + ([(3, (0, sector - 2))] if sector >= 2 else [])
    for sector in (2, 3):
        targets[3, sector] = [(2, sector - 2), (3, (1, sector - 2))]
    first, full, upper, tails = run_phase(
        [0, 1, 2],
        [(0, range(-2, OWN)), (1, range(OWN)), (2, (2, 3))],
        [window],
        sources,
        [(OWN,) + wide, (OWN,) + wide, (2,) + wide, (2, 2) + wide],
        targets,
        before_last,
        whole,
        part,
        mine,
        other,
    )
    bonds = [first[:, :, BLOCK:], full[:, :, BLOCK:]]
    for site in (2, 4, 6):
        tails = lax.ppermute(tails, ("x", "y0"), onward)
        last = site == 6
        if last:
            early = len(bonds)
            over = core_exchange(bonds)
        sources = {}
        for sector in (-2, -1):
            sources[site, sector] = (2, (0, sector + 2))
            sources[site + 1, sector] = (2, (1, sector + 2))
        for sector in range(OWN):
            sources[site, sector] = (0, sector)
        for sector in (2, 3):
            sources[site + 1, sector] = (1, sector - 2)
        targets = {}
        for sector in (0, 1):
            targets[site + 1, sector] = [(0, sector)]
        for sector in range(OWN):
            targets[site + 2, sector] = [(1, sector)]
        steps = [(site, (0, 1)), (site + 1, range(OWN))]
        outs = [(2,) + wide, (OWN,) + ((BLOCK, BLOCK) if last else wide)]
        if not last:
            for sector in (2, 3):
                targets[site + 2, sector].append((3, (0, sector - 2)))
                targets[site + 3, sector] = [(2, sector - 2), (3, (1, sector - 2))]
            steps.append((site + 2, (2, 3)))
            outs += [(2,) + wide, (2, 2) + wide]
        old_upper = upper
        lower, full, *rest = run_phase(
            [site, site + 1] + ([] if last else [site + 2]),
            steps,
            [full, upper, tails],
            sources,
            outs,
            targets,
            before_last,
            whole,
            part,
            mine,
            other,
        )
        bonds += [lower[:, :, BLOCK:], old_upper[:, :, BLOCK:], full if last else full[:, :, BLOCK:]]
        if not last:
            upper, tails = rest

    late = core_exchange(bonds[early:])
    summed = add_up(add_cores, (4, 2, 4, BLOCK // 2, BLOCK), over, late).reshape(32, BLOCK // 2, BLOCK)
    over = lax.all_to_all(summed, ("zhi", "zlo", "yl"), 0, 0)
    summed = add_up(add_columns, (BLOCK // 2, BLOCK), over)
    swapped = lax.ppermute(summed, ("zlo", "y0"), SWAP)
    return jnp.where(at_zlo == at_y0, summed, swapped)[None]


def solution(mesh):
    parts = Mesh(mesh.devices.reshape(4, 2, 4, 2, 4, 2), AXES)
    seg, op = ("zhi", "core"), ("x", "zlo", "yl", "y0")
    placed = (P(seg, None, None, None), P(op, None, None), P(op, None), P(op), P(op, None), P(op, None))
    return jax.shard_map(body, mesh=parts, in_specs=placed, out_specs=P(seg, op, None), check_vma=False)
```
